32 devices in a mesh: batch: 2 (over core), lon: 4 (over y, x), lat: 4 (over z).
Axes of the slice: x: 2, y: 2, z: 4, core: 2. Of those that a mesh axis runs over, the one named last changes fastest.
Arguments:
- imagery: bfloat16 [6, 512, 4096], P('batch', 'lat', 'lon'), parts along dimension 0, may hold values from -6 to 6
- stem_weight: bfloat16 [4, 768, 1024], replicated, may hold values from -0.109375 to 0.109375
- down_weight: bfloat16 [1024, 512], replicated, may hold values from -0.1875 to 0.1875
- height_qkv: bfloat16 [512, 1024], replicated, may hold values from -0.25 to 0.25
- height_bias: float32 [8, 63], replicated, may hold values from -1.5 to 301.5
- width_qkv: bfloat16 [512, 1024], replicated, may hold values from -0.25 to 0.25
- width_bias: float32 [8, 256], replicated, may hold values from -1.5 to 301.5
- up_weight: bfloat16 [512, 1024], replicated, may hold values from -0.25 to 0.25
Outputs:
- block_output: bfloat16 [64, 256, 1024], P(('batch', 'lat'), 'lon'), parts along dimension 0
The draws below stay inside these ranges and needn't reach their ends.
There are 2 independent parts, one for each index of `batch`. The reference program is written for one: setup_inputs(seed, part) draws one part's arguments, and reference() takes and returns one part's arrays. A program takes and returns all parts, laid end to end along the dimension named above; an argument that names none is the same for every part. Nothing has to cross between parts.
All inputs are finite; a program needn't handle non-finite values.
Results may differ from the reference program's by a relative error of at most 0.012.
Values may be sent and summed in bfloat16 or wider, within the bound.
A program may use at most 128 MiB of HBM per device.

```python
import jax
import jax.numpy as jnp
from jax import lax

C = 1024
QK = 256
VD = 512
HEADS = 8
PATCH = 16
DQ = 32
DV = 64
H = 32
W = 256
NY = 512
NX = 4096


def draw_height_bias(key, part):
    uniform_part = jax.random.uniform(jax.random.fold_in(key, 1), (HEADS, 2 * H - 1), jnp.float32, -1.5, 1.5)
    return uniform_part


def draw_width_bias(key, part):
    uniform_part = jax.random.uniform(jax.random.fold_in(key, 11), (HEADS, W), jnp.float32, -1.5, 1.5)
    return uniform_part


def block_levels(rng, shape, cuts, least, high):
    def one(axis_at, blocks):
        heights = jax.random.uniform(jax.random.fold_in(jax.random.fold_in(rng, 6), axis_at), (blocks,), jnp.float32, least / len(cuts), high / len(cuts))
        return jnp.repeat(jnp.exp(heights), shape[axis_at] // blocks).reshape((-1,) + (1,) * (len(shape) - axis_at - 1))

    gain = one(*cuts[0])
    for cut in cuts[1:]:
        gain = gain * one(*cut)
    return gain


def bell_draw(own_key, shape, spread, reach, cuts=(), kind=jnp.bfloat16):
    entries = jax.random.normal(own_key, shape, jnp.float32) * spread
    if len(cuts) > 0:
        entries = block_levels(own_key, shape, cuts, -0.22, 0.18) * entries
    return jnp.clip(entries, min=-reach, max=reach).astype(kind)


def setup_inputs(seed: int = 0, part: int = 0) -> dict:
    streams_of = jax.random.split(jax.random.key(seed), 9)
    own_keys = jax.random.split(jax.random.fold_in(streams_of[8], part), 9)
    return {
        "imagery": bell_draw(own_keys[0], (3, NY, NX), 1.0, 6.0, ((1, 4), (2, 4))),
        "stem_weight": bell_draw(streams_of[1], (4, 3 * PATCH * PATCH, C), (12 * PATCH * PATCH) ** -0.5, 0.109375),
        "down_weight": bell_draw(streams_of[2], (C, VD), C ** -0.5, 0.1875),
        "height_qkv": jnp.clip(jax.random.uniform(streams_of[3], (VD, 2 * QK + VD), jnp.float32, -0.25, 0.25), -0.25, 0.25).astype(jnp.bfloat16),
        "height_bias": draw_height_bias(jax.random.fold_in(streams_of[8], 71), part),
        "width_qkv": bell_draw(streams_of[5], (VD, 2 * QK + VD), VD ** -0.5, 0.25),
        "width_bias": draw_width_bias(jax.random.fold_in(streams_of[8], 71), part),
        "up_weight": bell_draw(streams_of[7], (VD, C), VD ** -0.5, 0.25),
    }


def stem_features(padded, stem_weight, map_rows, map_cols):
    channels = padded.shape[0]
    blocks = padded.reshape(channels, map_rows + 1, PATCH, map_cols + 1, PATCH)
    blocks = blocks.transpose(1, 3, 0, 2, 4).reshape(map_rows + 1, map_cols + 1, channels * PATCH * PATCH)
    summed = jnp.zeros((map_rows * map_cols, stem_weight.shape[2]), jnp.float32)
    for row_shift in range(2):
        for col_shift in range(2):
            window = blocks[row_shift:row_shift + map_rows, col_shift:col_shift + map_cols]
            window = window.reshape(map_rows * map_cols, channels * PATCH * PATCH)
            summed = summed + jnp.dot(window, stem_weight[2 * row_shift + col_shift], preferred_element_type=jnp.float32)
    return jax.nn.relu(summed).astype(jnp.bfloat16)


def head_attention(inputs):
    q_head, k_head, v_head, bias_head = inputs
    scores = jnp.einsum('pbd,obd->bpo', q_head, k_head) * (DQ ** -0.5) + bias_head[None]
    row_peak = jnp.max(scores, axis=-1, keepdims=True)
    weights = jnp.exp(scores - row_peak)
    denominator = jnp.sum(weights, axis=-1)
    rounded = lax.optimization_barrier(weights.astype(jnp.bfloat16)).astype(jnp.float32)
    weighted = jnp.einsum('bpo,obd->bpd', rounded, v_head)
    return weighted / denominator[..., None]


def axis_attention(projected, bias_full):
    extent = projected.shape[0]
    across = projected.shape[1]
    as_float = projected.astype(jnp.float32)
    q_all = as_float[..., :QK].reshape(extent, across, HEADS, DQ).transpose(2, 0, 1, 3)
    k_all = as_float[..., QK:2 * QK].reshape(extent, across, HEADS, DQ).transpose(2, 0, 1, 3)
    v_all = as_float[..., 2 * QK:].reshape(extent, across, HEADS, DV).transpose(2, 0, 1, 3)
    result = lax.map(head_attention, (q_all, k_all, v_all, bias_full))
    return result.transpose(2, 1, 0, 3).reshape(extent, across, VD).astype(jnp.bfloat16)


def reference(imagery, stem_weight, down_weight, height_qkv, height_bias, width_qkv, width_bias, up_weight):
    rim_width = PATCH // 2
    widened = jnp.concatenate([imagery[:, :, -rim_width:], imagery, imagery[:, :, :rim_width]], axis=2)
    padded = jnp.pad(widened, ((0, 0), (rim_width, rim_width), (0, 0)))
    features = stem_features(padded, stem_weight, H, W)
    middle = jax.nn.relu(jnp.dot(features, down_weight, preferred_element_type=jnp.float32)).astype(jnp.bfloat16)
    height_proj = jnp.dot(middle, height_qkv, preferred_element_type=jnp.float32).astype(jnp.bfloat16)
    height_proj = height_proj.reshape(H, W, 2 * QK + VD)
    row_index = jnp.arange(H, dtype=jnp.int32)
    height_offsets = row_index[None, :] - row_index[:, None] + H - 1
    height_full = jnp.take(height_bias, height_offsets, axis=1)
    height_out = axis_attention(height_proj, height_full)
    width_proj = jnp.dot(height_out.reshape(H * W, VD), width_qkv, preferred_element_type=jnp.float32).astype(jnp.bfloat16)
    width_proj = width_proj.reshape(H, W, 2 * QK + VD).transpose(1, 0, 2)
    col_index = jnp.arange(W, dtype=jnp.int32)
    width_offsets = (col_index[None, :] - col_index[:, None]) % W
    width_full = jnp.take(width_bias, width_offsets, axis=1)
    width_out = axis_attention(width_proj, width_full).transpose(1, 0, 2).reshape(H * W, VD)
    branch = jnp.dot(jax.nn.relu(width_out), up_weight, preferred_element_type=jnp.float32)
    result = jax.nn.relu(features.astype(jnp.float32) + branch).astype(jnp.bfloat16)
    return result.reshape(H, W, C)
```

```python
import functools

import jax
import jax.numpy as jnp
from jax import lax
from jax.experimental import pallas as pl
from jax.experimental.pallas import tpu as pltpu
from jax.sharding import PartitionSpec as P

QK = 256
VD = 512
HEADS = 8
PATCH = 16
DQ = 32
DV = 64


lowest_score = -1e30


def extended(cells, sides, width, closed):
    for axis, dim in sides:
        count = lax.axis_size(axis)
        ends = count if closed else count - 1
        head = lax.slice_in_dim(cells, 0, width, axis=dim)
        tail = lax.slice_in_dim(cells, cells.shape[dim] - width, cells.shape[dim], axis=dim)
        cells = jnp.concatenate(
            [
                lax.ppermute(tail, axis, [(i, (i + 1) % count) for i in range(ends)]),
                cells,
                lax.ppermute(head, axis, [((i + 1) % count, i) for i in range(ends)]),
            ],
            axis=dim,
        )
    return cells


def stem_features(padded, stem_weight, map_rows, map_cols):
    channels = padded.shape[0]
    blocks = padded.reshape(channels, map_rows + 1, PATCH, map_cols + 1, PATCH)
    blocks = blocks.transpose(1, 3, 0, 2, 4).reshape(
        map_rows + 1, map_cols + 1, channels * PATCH * PATCH
    )
    summed = jnp.zeros((map_rows * map_cols, stem_weight.shape[2]), jnp.float32)
    for row_shift in range(2):
        for col_shift in range(2):
            window = blocks[row_shift : row_shift + map_rows, col_shift : col_shift + map_cols]
            window = window.reshape(map_rows * map_cols, channels * PATCH * PATCH)
            summed = summed + jnp.dot(
                window, stem_weight[2 * row_shift + col_shift], preferred_element_type=jnp.float32
            )
    return jax.nn.relu(summed).astype(jnp.bfloat16)


def online_update(carried, scores, value_heads, form):
    running_max, denominator, weighted = carried
    new_peak = jnp.maximum(running_max, jnp.max(scores, axis=-1))
    weights = jnp.exp(scores - new_peak[..., None])
    denominator = jnp.sum(weights, axis=-1)
    weighted = jnp.einsum(
        form, weights.astype(jnp.bfloat16), value_heads, preferred_element_type=jnp.float32
    )
    return (new_peak, denominator, weighted)


def on_device(
    imagery, stem_weight, down_weight, height_qkv, height_bias, width_qkv, width_bias, up_weight
):
    rim_width = PATCH // 2
    widened = extended(imagery, (("lon", 2),), rim_width, True)
    padded = extended(widened, (("lat", 1),), rim_width, False)
    map_rows = imagery.shape[1] // PATCH
    map_cols = imagery.shape[2] // PATCH
    full_height = map_rows * lax.axis_size("lat")
    full_width = map_cols * lax.axis_size("lon")
    row_first = lax.axis_index("lat") * map_rows
    col_first = lax.axis_index("lon") * map_cols
    score_scale = DQ ** (-0.5)
    features = stem_features(padded, stem_weight, map_rows, map_cols)
    middle = jax.nn.relu(jnp.dot(features, down_weight, preferred_element_type=jnp.float32)).astype(
        jnp.bfloat16
    )
    height_proj = jnp.dot(middle, height_qkv, preferred_element_type=jnp.float32).astype(
        jnp.bfloat16
    )
    height_proj = height_proj.reshape(map_rows, map_cols, 2 * QK + VD)
    height_queries = height_proj[..., :QK].reshape(map_rows, map_cols, HEADS, DQ)
    initial = (
        jnp.full((HEADS, map_cols, map_rows), lowest_score, jnp.float32),
        jnp.zeros((HEADS, map_cols, map_rows), jnp.float32),
        jnp.zeros((HEADS, map_cols, map_rows, DV), jnp.float32),
    )
    key_rows = lax.all_gather(height_proj[..., QK : 2 * QK], "lat", axis=0, tiled=True)
    value_rows = lax.all_gather(height_proj[..., 2 * QK :], "lat", axis=0, tiled=True)
    key_count = key_rows.shape[0]
    scores = (
        jnp.einsum(
            "pwnd,ownd->nwpo",
            height_queries,
            key_rows.reshape(key_count, map_cols, HEADS, DQ),
            preferred_element_type=jnp.float32,
        )
        * score_scale
    )
    offsets = (
        jnp.arange(key_count, dtype=jnp.int32)[None, :]
        - (row_first + jnp.arange(map_rows, dtype=jnp.int32))[:, None]
        + full_height
        - 1
    )
    scores = scores + jnp.take(height_bias, offsets, axis=1)[:, None]
    running_max, denominator, weighted = online_update(
        initial, scores, value_rows.reshape(key_count, map_cols, HEADS, DV), "nwpo,ownd->nwpd"
    )
    height_out = (
        (weighted / denominator[..., None])
        .transpose(2, 1, 0, 3)
        .reshape(map_rows, map_cols, VD)
        .astype(jnp.bfloat16)
    )
    width_proj = jnp.dot(
        height_out.reshape(map_rows * map_cols, VD), width_qkv, preferred_element_type=jnp.float32
    ).astype(jnp.bfloat16)
    width_proj = width_proj.reshape(map_rows, map_cols, 2 * QK + VD)
    width_queries = width_proj[..., :QK].reshape(map_rows, map_cols, HEADS, DQ)
    width_initial = (
        jnp.full((HEADS, map_rows, map_cols), lowest_score, jnp.float32),
        jnp.zeros((HEADS, map_rows, map_cols), jnp.float32),
        jnp.zeros((HEADS, map_rows, map_cols, DV), jnp.float32),
    )
    key_cols = lax.all_gather(width_proj[..., QK : 2 * QK], "lon", axis=1, tiled=True)
    value_cols = lax.all_gather(width_proj[..., 2 * QK :], "lon", axis=1, tiled=True)
    key_count = key_cols.shape[1]
    scores = (
        jnp.einsum(
            "hwnd,hknd->nhwk",
            width_queries,
            key_cols.reshape(map_rows, key_count, HEADS, DQ),
            preferred_element_type=jnp.float32,
        )
        * score_scale
    )
    offsets = (
        jnp.arange(key_count, dtype=jnp.int32)[None, :]
        - (col_first + jnp.arange(map_cols, dtype=jnp.int32))[:, None]
    ) % full_width
    scores = scores + jnp.take(width_bias, offsets, axis=1)[:, None]
    width_max, width_denominator, width_weighted = online_update(
        width_initial, scores, value_cols.reshape(map_rows, key_count, HEADS, DV), "nhwk,hknd->nhwd"
    )
    width_out = (
        (width_weighted / width_denominator[..., None])
        .transpose(1, 2, 0, 3)
        .reshape(map_rows * map_cols, VD)
        .astype(jnp.bfloat16)
    )
    branch = jnp.dot(jax.nn.relu(width_out), up_weight, preferred_element_type=jnp.float32)
    result = jax.nn.relu(features.astype(jnp.float32) + branch).astype(jnp.bfloat16)
    return result.reshape(map_rows, map_cols, up_weight.shape[1])


MESH = pl.DeviceIdType.MESH
ANY = pl.BlockSpec(memory_space=pl.ANY)
VMEM = pl.BlockSpec(memory_space=pltpu.VMEM)
BLOCK = 128
VMEM_BYTES = 56 * 1024 * 1024


def greet(lats, lons):
    lat, lon = lax.axis_index("lat"), lax.axis_index("lon")
    barrier = pltpu.get_barrier_semaphore()

    def signal(step, carry):
        there = lax.rem(lon * lats + lat + step, lats * lons)
        pl.semaphore_signal(
            barrier,
            inc=1,
            device_id={"lat": lax.rem(there, lats), "lon": there // lats},
            device_id_type=MESH,
        )
        return carry

    lax.fori_loop(1, lats * lons, signal, 0)
    return barrier


def chunks_turned(tile, to_bands, pick, to_rows):
    turned = jnp.take_along_axis(tile, to_bands, axis=1, mode="promise_in_bounds")
    turned = jnp.take_along_axis(turned, pick, axis=0, mode="promise_in_bounds")
    return jnp.take_along_axis(turned, to_rows, axis=1, mode="promise_in_bounds")


def stem_kernel(
    lats, lons, img, stem_hbm, down_hbm, feat_ref, mid_ref,
    ext, stem_w, down_w, xs, outbox, inbox,
    load_sems, halo_send, halo_recv, send_sems, recv_sems,
):
    lat, lon = lax.axis_index("lat"), lax.axis_index("lon")
    barrier = greet(lats, lons)
    rows, cols = img.shape[1], img.shape[2]
    local = pltpu.make_async_copy(
        img, ext.at[:, pl.ds(16, rows), pl.ds(128, cols)], load_sems.at[0]
    )
    local.start()
    load_stem = pltpu.make_async_copy(stem_hbm, stem_w, load_sems.at[1])
    load_stem.start()
    load_down = pltpu.make_async_copy(down_hbm, down_w, load_sems.at[2])
    load_down.start()
    west, east = lax.rem(lon + lons - 1, lons), lax.rem(lon + 1, lons)

    @pl.when(lat == 0)
    def _():
        ext[:, 0:16, :] = jnp.zeros((3, 16, cols + 256), ext.dtype)

    @pl.when(lat == lats - 1)
    def _():
        ext[:, rows + 16 : rows + 32, :] = jnp.zeros((3, 16, cols + 256), ext.dtype)

    row_moves = {-1: (0, rows + 16, 16), 0: (0, 16, rows), 1: (rows - 16, 0, 16)}
    col_moves = {-1: (0, cols + 128, 128), 0: (0, 128, cols), 1: (cols - 128, 0, 128)}
    copies = []
    for down in (0, -1, 1):
        for right in (-1, 1, 0):
            if down == 0 and right == 0:
                continue
            y_from, y_to, y_size = row_moves[down]
            x_from, x_to, x_size = col_moves[right]
            slot = len(copies)
            copy = pltpu.make_async_remote_copy(
                src_ref=img.at[:, pl.ds(y_from, y_size), pl.ds(x_from, x_size)],
                dst_ref=ext.at[:, pl.ds(y_to, y_size), pl.ds(x_to, x_size)],
                send_sem=halo_send.at[slot],
                recv_sem=halo_recv.at[slot],
                device_id={
                    "lat": lax.rem(lat + down + lats, lats),
                    "lon": {-1: west, 0: lon, 1: east}[right],
                },
                device_id_type=MESH,
            )
            copies.append((down, copy))
    pl.semaphore_wait(barrier, lats * lons - 1)
    for down, copy in copies:
        if down == 0:
            copy.start()
        elif down == -1:
            pl.when(lat > 0)(copy.start)
        else:
            pl.when(lat < lats - 1)(copy.start)
    local.wait()
    for down, copy in copies:
        if down == 0:
            copy.wait_send()
            copy.wait_recv()
        elif down == -1:
            pl.when(lat > 0)(copy.wait_send)
            pl.when(lat < lats - 1)(copy.wait_recv)
        else:
            pl.when(lat < lats - 1)(copy.wait_send)
            pl.when(lat > 0)(copy.wait_recv)

    lane = lax.broadcasted_iota(jnp.int32, (8, 128), 1)
    sub = lax.broadcasted_iota(jnp.int32, (8, 128), 0)
    to_bands = lax.rem(lane - 16 * sub + 128, 128)
    pick = lax.rem(lane // 16 - sub + 8, 8)
    to_rows = lax.rem(lane + 16 * sub, 128)
    map_rows = rows // PATCH
    tiles = cols // 128 + 1

    def patch(i, carry):
        for c in range(3):
            slab = ext[c, pl.ds(pl.multiple_of(16 * i, 16), 32), :].astype(jnp.float32)
            for half in range(2):
                part = slab[8 + 8 * half : 16 + 8 * half, 120 : 120 + 128 * tiles]
                for t in range(tiles):
                    xs[i, 8 * t : 8 * t + 8, (2 * c + half) * 128 : (2 * c + half + 1) * 128] = (
                        chunks_turned(part[:, 128 * t : 128 * t + 128], to_bands, pick, to_rows)
                    )
        return carry

    lax.fori_loop(0, map_rows + 1, patch, 0)
    load_stem.wait()
    load_down.wait()
    width = cols // PATCH // lats
    depth = 3 * PATCH * PATCH

    def sending(dest, k):
        return pltpu.make_async_remote_copy(
            src_ref=outbox.at[dest],
            dst_ref=inbox.at[lat],
            send_sem=send_sems.at[k],
            recv_sem=recv_sems.at[k],
            device_id={"lat": dest, "lon": lon},
            device_id_type=MESH,
        )

    def group(k, carry):
        dest = lax.rem(lat + k, lats)
        first = pl.multiple_of(dest * width, width)
        here = xs[:, pl.ds(first, width + 8), :]
        x0 = here[:, :width, :].reshape((map_rows + 1) * width, depth).astype(jnp.bfloat16)
        x1 = here[:, 1 : width + 1, :].reshape((map_rows + 1) * width, depth).astype(jnp.bfloat16)
        count = map_rows * width
        total = jnp.dot(x0[:count], stem_w[0], preferred_element_type=jnp.float32)
        total += jnp.dot(x1[:count], stem_w[1], preferred_element_type=jnp.float32)
        total += jnp.dot(x0[width:], stem_w[2], preferred_element_type=jnp.float32)
        total += jnp.dot(x1[width:], stem_w[3], preferred_element_type=jnp.float32)
        feats = jnp.maximum(total, 0.0).astype(jnp.bfloat16)
        feat_ref[dest] = feats
        middle = jnp.dot(feats, down_w[...], preferred_element_type=jnp.float32)
        middle = jnp.maximum(middle, 0.0).astype(jnp.bfloat16)

        @pl.when(k < lats)
        def _():
            outbox[dest] = middle
            sending(dest, k).start()

        @pl.when(k == lats)
        def _():
            inbox[lat] = middle

        return carry

    lax.fori_loop(1, lats + 1, group, 0)

    def finish(k, carry):
        sending(lax.rem(lat + k, lats), k).wait()
        return carry

    lax.fori_loop(1, lats, finish, 0)
    mid_ref[...] = inbox[...]


def softmaxed(q, k, v, bias):
    count = q.shape[0]
    lane = lax.broadcasted_iota(jnp.int32, (count, QK), 1) // DQ
    pair_lane = lax.broadcasted_iota(jnp.int32, (count, 2 * DV), 1) // DV
    outs = []
    for pair in range(HEADS // 2):
        halves = []
        for n in (2 * pair, 2 * pair + 1):
            q_head = jnp.where(lane == n, q, jnp.zeros_like(q))
            scores = lax.dot_general(
                q_head, k, (((1,), (1,)), ((), ())), preferred_element_type=jnp.float32
            )
            scores = scores * (DQ ** (-0.5)) + bias[n]
            weights = jnp.exp(scores - jnp.max(scores, axis=-1, keepdims=True))
            denominator = jnp.sum(weights, axis=-1, keepdims=True)
            weighted = jnp.dot(
                weights.astype(jnp.bfloat16),
                v[:, 2 * DV * pair : 2 * DV * (pair + 1)],
                preferred_element_type=jnp.float32,
            )
            halves.append(weighted / denominator)
        outs.append(jnp.where(pair_lane == 0, halves[0], halves[1]))
    return jnp.concatenate(outs, axis=1)


def height_kernel(
    lats, lons, mid_ref, qkv_ref, bias_ref, row_ref,
    bias, proj, result, outbox, inbox, send_sems, recv_sems,
):
    lat, lon = lax.axis_index("lat"), lax.axis_index("lon")
    barrier = greet(lats, lons)
    positions = mid_ref.shape[0] * mid_ref.shape[1]
    width = inbox.shape[1] // (lats * lons)
    height = positions // width
    own_rows = inbox.shape[0]
    beside = BLOCK // height
    i = lax.broadcasted_iota(jnp.int32, (BLOCK, BLOCK), 0)
    j = lax.broadcasted_iota(jnp.int32, (BLOCK, BLOCK), 1)
    for n in range(HEADS):
        spread = jnp.broadcast_to(bias_ref[n : n + 1, :], (BLOCK, BLOCK))
        turned = pltpu.roll(spread, BLOCK - (height - 1), 1, stride=1, stride_axis=0)
        bias[n] = jnp.where(i // height == j // height, turned, lowest_score)
    projected = jnp.dot(
        mid_ref[...].reshape(positions, VD), qkv_ref[...], preferred_element_type=jnp.float32
    )
    for c in range(proj.shape[0]):
        proj[c] = projected[:, 128 * c : 128 * c + 128]

    def block(g, carry):
        parts = [
            jnp.concatenate(
                [
                    proj[c, pl.ds(g * beside + w, height, stride=width), :]
                    for c in range(proj.shape[0])
                ],
                axis=1,
            )
            for w in range(beside)
        ]
        mine = jnp.concatenate(parts, axis=0).astype(jnp.bfloat16)
        out = softmaxed(mine[:, :QK], mine[:, QK : 2 * QK], mine[:, 2 * QK :], bias)
        for w in range(beside):
            for c in range(result.shape[0]):
                result[c, pl.ds(g * beside + w, height, stride=width), :] = out[
                    w * height : (w + 1) * height, 128 * c : 128 * c + 128
                ]
        return carry

    lax.fori_loop(0, width // beside, block, 0)
    for c in range(result.shape[0]):
        outbox[:, :, :, 128 * c : 128 * c + 128] = (
            result[c].astype(jnp.bfloat16).reshape(outbox.shape[:3] + (128,))
        )
    pl.semaphore_wait(barrier, lats * lons - 1)
    me = lat * lons + lon
    others = lats * lons
    column = pl.multiple_of((lon * lats + lat) * width, width)

    def sending(k):
        there = lax.rem(me + k, others)
        return pltpu.make_async_remote_copy(
            src_ref=outbox.at[there],
            dst_ref=inbox.at[:, pl.ds(column, width), :],
            send_sem=send_sems.at[k],
            recv_sem=recv_sems.at[k],
            device_id={"lat": there // lons, "lon": lax.rem(there, lons)},
            device_id_type=MESH,
        )

    def start(k, carry):
        sending(k).start()
        return carry

    lax.fori_loop(1, others, start, 0)
    inbox[:, pl.ds(column, width), :] = outbox[me]

    def finish(k, carry):
        sending(k).wait()
        return carry

    lax.fori_loop(1, others, finish, 0)
    row_ref[...] = inbox[...]


def width_kernel(
    lats, lons, row_ref, qkv_ref, bias_ref, wide_ref,
    bias, outbox, inbox, send_sems, recv_sems,
):
    lon = lax.axis_index("lon")
    barrier = pltpu.get_barrier_semaphore()
    for k in range(1, lons):
        pl.semaphore_signal(
            barrier, inc=1, device_id={"lon": lax.rem(lon + k, lons)}, device_id_type=MESH
        )
    own_rows, full, _ = row_ref.shape
    for n in range(HEADS):
        spread = jnp.broadcast_to(bias_ref[n : n + 1, :], (full, full))
        bias[n] = pltpu.roll(spread, 0, 1, stride=1, stride_axis=0)
    part = full // lons

    def row(r, carry):
        mine = jnp.dot(row_ref[r], qkv_ref[...], preferred_element_type=jnp.float32).astype(
            jnp.bfloat16
        )
        out = softmaxed(mine[:, :QK], mine[:, QK : 2 * QK], mine[:, 2 * QK :], bias)
        out = jnp.maximum(out, 0.0).astype(jnp.bfloat16)
        for d in range(lons):
            outbox[d, r] = out[part * d : part * (d + 1)]
        return carry

    lax.fori_loop(0, own_rows, row, 0)
    pl.semaphore_wait(barrier, lons - 1)

    def sending(k):
        there = lax.rem(lon + k, lons)
        return pltpu.make_async_remote_copy(
            src_ref=outbox.at[there],
            dst_ref=inbox.at[lon],
            send_sem=send_sems.at[k],
            recv_sem=recv_sems.at[k],
            device_id={"lon": there},
            device_id_type=MESH,
        )

    for k in range(1, lons):
        sending(k).start()
    inbox[lon] = outbox[lon]
    for k in range(1, lons):
        sending(k).wait()
    wide_ref[...] = inbox[...]


def up_kernel(lats, wide_ref, feat_ref, up_ref, out_ref):
    map_rows, map_cols, channels = out_ref.shape
    width = map_cols // lats
    for k in range(lats):
        x = wide_ref[:, k * width : (k + 1) * width, :].reshape(map_rows * width, VD)
        branch = jnp.dot(x, up_ref[...], preferred_element_type=jnp.float32)
        total = jnp.maximum(feat_ref[k].astype(jnp.float32) + branch, 0.0)
        out_ref[:, k * width : (k + 1) * width, :] = total.astype(jnp.bfloat16).reshape(
            map_rows, width, channels
        )


def with_kernels(
    imagery, stem_weight, down_weight, height_qkv, height_bias, width_qkv, width_bias, up_weight
):
    lats, lons = lax.axis_size("lat"), lax.axis_size("lon")
    bf16, f32 = jnp.bfloat16, jnp.float32
    _, rows, cols = imagery.shape
    map_rows, map_cols = rows // PATCH, cols // PATCH
    positions = map_rows * map_cols
    channels = stem_weight.shape[2]
    full_height, full_width = map_rows * lats, map_cols * lons
    depth = stem_weight.shape[1]
    width = map_cols // lats
    own_rows = map_rows // lons
    dma = pltpu.SemaphoreType.DMA

    def params(number):
        return pltpu.CompilerParams(
            collective_id=number, has_side_effects=True, vmem_limit_bytes=VMEM_BYTES
        )

    feats, mid = pl.pallas_call(
        functools.partial(stem_kernel, lats, lons),
        name="stem",
        out_shape=(
            jax.ShapeDtypeStruct((lats, positions // lats, channels), bf16),
            jax.ShapeDtypeStruct((lats, positions // lats, VD), bf16),
        ),
        in_specs=[ANY] * 3,
        out_specs=(VMEM, VMEM),
        scratch_shapes=[
            pltpu.VMEM((3, rows + 32, cols + 256), bf16),
            pltpu.VMEM(stem_weight.shape, bf16),
            pltpu.VMEM(down_weight.shape, bf16),
            pltpu.VMEM((map_rows + 1, map_cols + 8, depth), f32),
            pltpu.VMEM((lats, positions // lats, VD), bf16),
            pltpu.VMEM((lats, positions // lats, VD), bf16),
            dma((3,)),
            dma((8,)),
            dma((8,)),
            dma((lats,)),
            dma((lats,)),
        ],
        compiler_params=params(0),
    )(imagery, stem_weight, down_weight)
    spread_bias = jnp.pad(height_bias, ((0, 0), (0, BLOCK - height_bias.shape[1])))
    row = pl.pallas_call(
        functools.partial(height_kernel, lats, lons),
        name="height",
        out_shape=jax.ShapeDtypeStruct((own_rows, full_width, VD), bf16),
        in_specs=[VMEM] * 3,
        out_specs=VMEM,
        scratch_shapes=[
            pltpu.VMEM((HEADS, BLOCK, BLOCK), f32),
            pltpu.VMEM(((2 * QK + VD) // 128, positions, 128), f32),
            pltpu.VMEM((VD // 128, positions, 128), f32),
            pltpu.VMEM((lats * lons, own_rows, width, VD), bf16),
            pltpu.VMEM((own_rows, full_width, VD), bf16),
            dma((lats * lons,)),
            dma((lats * lons,)),
        ],
        compiler_params=params(1),
    )(mid, height_qkv, spread_bias)
    wide = pl.pallas_call(
        functools.partial(width_kernel, lats, lons),
        name="width",
        out_shape=jax.ShapeDtypeStruct((lons, own_rows, map_cols, VD), bf16),
        in_specs=[VMEM] * 3,
        out_specs=VMEM,
        scratch_shapes=[
            pltpu.VMEM((HEADS, full_width, full_width), f32),
            pltpu.VMEM((lons, own_rows, map_cols, VD), bf16),
            pltpu.VMEM((lons, own_rows, map_cols, VD), bf16),
            dma((lons,)),
            dma((lons,)),
        ],
        compiler_params=params(2),
    )(row, width_qkv, width_bias)
    return pl.pallas_call(
        functools.partial(up_kernel, lats),
        name="up",
        out_shape=jax.ShapeDtypeStruct((map_rows, map_cols, channels), bf16),
        in_specs=[VMEM] * 3,
        out_specs=VMEM,
        compiler_params=pltpu.CompilerParams(vmem_limit_bytes=VMEM_BYTES),
    )(wide.reshape(map_rows, map_cols, VD), feats, up_weight)


def either(*args):
    lats, lons = lax.axis_size("lat"), lax.axis_size("lon")
    _, rows, cols = args[0].shape
    map_rows, map_cols = rows // PATCH, cols // PATCH
    whole_tiles = (
        map_cols % (16 * lats) == 0
        and map_rows % lons == 0
        and BLOCK % (map_rows * lats) == 0
        and 2 * map_rows * lats - 1 <= BLOCK
        and (map_cols // lats) % (BLOCK // (map_rows * lats)) == 0
        and cols % 128 == 0
        and map_rows % 8 == 0
    )
    return with_kernels(*args) if whole_tiles else on_device(*args)


def solution(mesh):
    placed = (P("batch", "lat", "lon"), P(), P(), P(), P(), P(), P(), P())
    return jax.shard_map(
        either,
        mesh=mesh,
        in_specs=placed,
        out_specs=P(("batch", "lat"), "lon", None),
        check_vma=False,
    )
```

```python
import functools

import jax
import jax.numpy as jnp
from jax import lax
from jax.experimental import pallas as pl
from jax.experimental.pallas import tpu as pltpu
from jax.sharding import PartitionSpec as P

QK = 256
VD = 512
HEADS = 8
PATCH = 16
DQ = 32
DV = 64


lowest_score = -1e30


def extended(cells, sides, width, closed):
    for axis, dim in sides:
        count = lax.axis_size(axis)
        ends = count if closed else count - 1
        head = lax.slice_in_dim(cells, 0, width, axis=dim)
        tail = lax.slice_in_dim(cells, cells.shape[dim] - width, cells.shape[dim], axis=dim)
        cells = jnp.concatenate(
            [
                lax.ppermute(tail, axis, [(i, (i + 1) % count) for i in range(ends)]),
                cells,
                lax.ppermute(head, axis, [((i + 1) % count, i) for i in range(ends)]),
            ],
            axis=dim,
        )
    return cells


def stem_features(padded, stem_weight, map_rows, map_cols):
    channels = padded.shape[0]
    blocks = padded.reshape(channels, map_rows + 1, PATCH, map_cols + 1, PATCH)
    blocks = blocks.transpose(1, 3, 0, 2, 4).reshape(
        map_rows + 1, map_cols + 1, channels * PATCH * PATCH
    )
    summed = jnp.zeros((map_rows * map_cols, stem_weight.shape[2]), jnp.float32)
    for row_shift in range(2):
        for col_shift in range(2):
            window = blocks[row_shift : row_shift + map_rows, col_shift : col_shift + map_cols]
            window = window.reshape(map_rows * map_cols, channels * PATCH * PATCH)
            summed = summed + jnp.dot(
                window, stem_weight[2 * row_shift + col_shift], preferred_element_type=jnp.float32
            )
    return jax.nn.relu(summed).astype(jnp.bfloat16)


def online_update(carried, scores, value_heads, form):
    running_max, denominator, weighted = carried
    new_peak = jnp.maximum(running_max, jnp.max(scores, axis=-1))
    weights = jnp.exp(scores - new_peak[..., None])
    denominator = jnp.sum(weights, axis=-1)
    weighted = jnp.einsum(
        form, weights.astype(jnp.bfloat16), value_heads, preferred_element_type=jnp.float32
    )
    return (new_peak, denominator, weighted)


def on_device(
    imagery, stem_weight, down_weight, height_qkv, height_bias, width_qkv, width_bias, up_weight
):
    rim_width = PATCH // 2
    widened = extended(imagery, (("lon", 2),), rim_width, True)
    padded = extended(widened, (("lat", 1),), rim_width, False)
    map_rows = imagery.shape[1] // PATCH
    map_cols = imagery.shape[2] // PATCH
    full_height = map_rows * lax.axis_size("lat")
    full_width = map_cols * lax.axis_size("lon")
    row_first = lax.axis_index("lat") * map_rows
    col_first = lax.axis_index("lon") * map_cols
    score_scale = DQ ** (-0.5)
    features = stem_features(padded, stem_weight, map_rows, map_cols)
    middle = jax.nn.relu(jnp.dot(features, down_weight, preferred_element_type=jnp.float32)).astype(
        jnp.bfloat16
    )
    height_proj = jnp.dot(middle, height_qkv, preferred_element_type=jnp.float32).astype(
        jnp.bfloat16
    )
    height_proj = height_proj.reshape(map_rows, map_cols, 2 * QK + VD)
    height_queries = height_proj[..., :QK].reshape(map_rows, map_cols, HEADS, DQ)
    initial = (
        jnp.full((HEADS, map_cols, map_rows), lowest_score, jnp.float32),
        jnp.zeros((HEADS, map_cols, map_rows), jnp.float32),
        jnp.zeros((HEADS, map_cols, map_rows, DV), jnp.float32),
    )
    key_rows = lax.all_gather(height_proj[..., QK : 2 * QK], "lat", axis=0, tiled=True)
    value_rows = lax.all_gather(height_proj[..., 2 * QK :], "lat", axis=0, tiled=True)
    key_count = key_rows.shape[0]
    scores = (
        jnp.einsum(
            "pwnd,ownd->nwpo",
            height_queries,
            key_rows.reshape(key_count, map_cols, HEADS, DQ),
            preferred_element_type=jnp.float32,
        )
        * score_scale
    )
    offsets = (
        jnp.arange(key_count, dtype=jnp.int32)[None, :]
        - (row_first + jnp.arange(map_rows, dtype=jnp.int32))[:, None]
        + full_height
        - 1
    )
    scores = scores + jnp.take(height_bias, offsets, axis=1)[:, None]
    running_max, denominator, weighted = online_update(
        initial, scores, value_rows.reshape(key_count, map_cols, HEADS, DV), "nwpo,ownd->nwpd"
    )
    height_out = (
        (weighted / denominator[..., None])
        .transpose(2, 1, 0, 3)
        .reshape(map_rows, map_cols, VD)
        .astype(jnp.bfloat16)
    )
    width_proj = jnp.dot(
        height_out.reshape(map_rows * map_cols, VD), width_qkv, preferred_element_type=jnp.float32
    ).astype(jnp.bfloat16)
    width_proj = width_proj.reshape(map_rows, map_cols, 2 * QK + VD)
    width_queries = width_proj[..., :QK].reshape(map_rows, map_cols, HEADS, DQ)
    width_initial = (
        jnp.full((HEADS, map_rows, map_cols), lowest_score, jnp.float32),
        jnp.zeros((HEADS, map_rows, map_cols), jnp.float32),
        jnp.zeros((HEADS, map_rows, map_cols, DV), jnp.float32),
    )
    key_cols = lax.all_gather(width_proj[..., QK : 2 * QK], "lon", axis=1, tiled=True)
    value_cols = lax.all_gather(width_proj[..., 2 * QK :], "lon", axis=1, tiled=True)
    key_count = key_cols.shape[1]
    scores = (
        jnp.einsum(
            "hwnd,hknd->nhwk",
            width_queries,
            key_cols.reshape(map_rows, key_count, HEADS, DQ),
            preferred_element_type=jnp.float32,
        )
        * score_scale
    )
    offsets = (
        jnp.arange(key_count, dtype=jnp.int32)[None, :]
        - (col_first + jnp.arange(map_cols, dtype=jnp.int32))[:, None]
    ) % full_width
    scores = scores + jnp.take(width_bias, offsets, axis=1)[:, None]
    width_max, width_denominator, width_weighted = online_update(
        width_initial, scores, value_cols.reshape(map_rows, key_count, HEADS, DV), "nhwk,hknd->nhwd"
    )
    width_out = (
        (width_weighted / width_denominator[..., None])
        .transpose(1, 2, 0, 3)
        .reshape(map_rows * map_cols, VD)
        .astype(jnp.bfloat16)
    )
    branch = jnp.dot(jax.nn.relu(width_out), up_weight, preferred_element_type=jnp.float32)
    result = jax.nn.relu(features.astype(jnp.float32) + branch).astype(jnp.bfloat16)
    return result.reshape(map_rows, map_cols, up_weight.shape[1])


MESH = pl.DeviceIdType.MESH
ANY = pl.BlockSpec(memory_space=pl.ANY)
VMEM = pl.BlockSpec(memory_space=pltpu.VMEM)
BLOCK = 128
HALVES = 2
VMEM_BYTES = 58 * 1024 * 1024
LOG2E = 1.4426950408889634


def chunks_turned(tile, to_bands, pick, to_rows):
    turned = jnp.take_along_axis(tile, to_bands, axis=1, mode="promise_in_bounds")
    turned = jnp.take_along_axis(turned, pick, axis=0, mode="promise_in_bounds")
    return jnp.take_along_axis(turned, to_rows, axis=1, mode="promise_in_bounds")


def attention(q, k, v, bias):
    count = q.shape[0]
    lane = lax.broadcasted_iota(jnp.int32, (count, QK), 1) // DQ
    first = lax.broadcasted_iota(jnp.int32, (count, 2 * DV), 1) < DV
    outs = []
    for pair in range(HEADS // 2):
        values = v[:, 2 * DV * pair : 2 * DV * (pair + 1)]
        ones = jnp.ones_like(values)
        both = []
        for n in (2 * pair, 2 * pair + 1):
            q_head = jnp.where(lane == n, q, jnp.zeros_like(q))
            scores = lax.dot_general(
                q_head, k, (((1,), (1,)), ((), ())), preferred_element_type=jnp.float32
            )
            scores = scores * (DQ ** (-0.5) * LOG2E) + bias[n]
            weights = jnp.exp2(scores - jnp.max(scores, axis=-1, keepdims=True))
            held = jnp.where(first, values, ones) if n % 2 == 0 else jnp.where(first, ones, values)
            both.append(
                jnp.dot(weights.astype(jnp.bfloat16), held, preferred_element_type=jnp.float32)
            )
        totals = pltpu.roll(jnp.where(first, both[1], both[0]), DV, 1)
        outs.append(jnp.where(first, both[0], both[1]) / totals)
    return jnp.concatenate(outs, axis=1)


def block_kernel(
    lats, lons, img, stem_hbm, down_hbm, height_hbm, width_hbm, up_hbm, height_bias, width_bias,
    out_ref,
    ext, stem_w, down_w, height_w, width_w, up_w, xs, feats, padded_bias, bias_h, bias_w,
    proj_h, result, proj_w, out_a, in_a, out_b, in_b, out_c, in_c,
    load_sems, halo_send, halo_recv, send_a, recv_a, send_b, recv_b, send_c, recv_c,
):
    lat, lon = lax.axis_index("lat"), lax.axis_index("lon")
    rows, cols = img.shape[1], img.shape[2]
    map_rows, map_cols = rows // PATCH, cols // PATCH
    full_height, full_width = map_rows * lats, map_cols * lons
    width = map_cols // lats
    own_rows = map_rows // lons
    depth = 3 * PATCH * PATCH
    others = lats * lons

    barrier = pltpu.get_barrier_semaphore()

    def greet(step, carry):
        there = lax.rem(lon * lats + lat + step, others)
        pl.semaphore_signal(
            barrier,
            inc=1,
            device_id={"lat": lax.rem(there, lats), "lon": there // lats},
            device_id_type=MESH,
        )
        return carry

    lax.fori_loop(1, others, greet, 0)
    local = pltpu.make_async_copy(
        img, ext.at[:, pl.ds(16, rows), pl.ds(128, cols)], load_sems.at[0]
    )
    local.start()
    loads = []
    for number, (source, held) in enumerate(
        (
            (stem_hbm, stem_w),
            (down_hbm, down_w),
            (height_hbm, height_w),
            (width_hbm, width_w),
            (up_hbm, up_w),
        )
    ):
        loads.append(pltpu.make_async_copy(source, held, load_sems.at[number + 1]))
        loads[-1].start()
    west, east = lax.rem(lon + lons - 1, lons), lax.rem(lon + 1, lons)

    @pl.when(lat == 0)
    def _():
        ext[:, 0:16, :] = jnp.zeros((3, 16, cols + 256), ext.dtype)

    @pl.when(lat == lats - 1)
    def _():
        ext[:, rows + 16 : rows + 32, :] = jnp.zeros((3, 16, cols + 256), ext.dtype)

    row_moves = {-1: (0, rows + 16, 16), 0: (0, 16, rows), 1: (rows - 16, 0, 16)}
    col_moves = {-1: (0, cols + 128, 128), 0: (0, 128, cols), 1: (cols - 128, 0, 128)}
    copies = []
    for down, right in ((-1, 0), (1, 0), (0, -1), (0, 1), (-1, -1), (-1, 1), (1, -1), (1, 1)):
        y_from, y_to, y_size = row_moves[down]
        x_from, x_to, x_size = col_moves[right]
        slot = len(copies)
        copy = pltpu.make_async_remote_copy(
            src_ref=img.at[:, pl.ds(y_from, y_size), pl.ds(x_from, x_size)],
            dst_ref=ext.at[:, pl.ds(y_to, y_size), pl.ds(x_to, x_size)],
            send_sem=halo_send.at[slot],
            recv_sem=halo_recv.at[slot],
            device_id={
                "lat": lax.rem(lat + down + lats, lats),
                "lon": {-1: west, 0: lon, 1: east}[right],
            },
            device_id_type=MESH,
        )
        copies.append((down, copy))
    pl.semaphore_wait(barrier, others - 1)
    for down, copy in copies:
        if down == 0:
            copy.start()
        elif down == -1:
            pl.when(lat > 0)(copy.start)
        else:
            pl.when(lat < lats - 1)(copy.start)

    lane = lax.broadcasted_iota(jnp.int32, (8, 128), 1)
    sub = lax.broadcasted_iota(jnp.int32, (8, 128), 0)
    to_bands = lax.rem(lane - 16 * sub + 128, 128)
    pick = lax.rem(lane // 16 - sub + 8, 8)
    to_rows = lax.rem(lane + 16 * sub, 128)
    tiles = cols // 128 + 1

    def patch(i, first, count):
        for c in range(3):
            slab = ext[
                c,
                pl.ds(pl.multiple_of(16 * i, 16), 32),
                128 * first : 128 * (first + count + 1),
            ].astype(jnp.float32)
            for half in range(2):
                part = slab[8 + 8 * half : 16 + 8 * half, 120 : 120 + 128 * count]
                for t in range(count):
                    at = 8 * (first + t)
                    xs[i, at : at + 8, (2 * c + half) * 128 : (2 * c + half + 1) * 128] = (
                        chunks_turned(part[:, 128 * t : 128 * t + 128], to_bands, pick, to_rows)
                    )

    def inner(i, carry):
        patch(i, 1, tiles - 2)
        return carry

    def rim(i, carry):
        patch(i, 0, 1)
        patch(i, tiles - 1, 1)
        return carry

    local.wait()
    lax.fori_loop(1, map_rows, inner, 0)

    padded_bias[...] = jnp.zeros(padded_bias.shape, jnp.float32)
    padded_bias[:, 0 : height_bias.shape[1]] = height_bias[...]
    down_row = lax.broadcasted_iota(jnp.int32, (BLOCK, BLOCK), 0) // full_height
    key_row = lax.broadcasted_iota(jnp.int32, (BLOCK, BLOCK), 1) // full_height
    for n in range(HEADS):
        spread = jnp.broadcast_to(padded_bias[n : n + 1, :] * LOG2E, (BLOCK, BLOCK))
        turned = pltpu.roll(spread, BLOCK - (full_height - 1), 1, stride=1, stride_axis=0)
        bias_h[n] = jnp.where(down_row == key_row, turned, lowest_score)
        spread = jnp.broadcast_to(width_bias[n : n + 1, :] * LOG2E, (full_width, full_width))
        bias_w[n] = pltpu.roll(spread, 0, 1, stride=1, stride_axis=0)

    for down, copy in copies:
        if down == 0:
            copy.wait_send()
            copy.wait_recv()
        elif down == -1:
            pl.when(lat > 0)(copy.wait_send)
            pl.when(lat < lats - 1)(copy.wait_recv)
        else:
            pl.when(lat < lats - 1)(copy.wait_send)
            pl.when(lat > 0)(copy.wait_recv)
    patch(0, 1, tiles - 2)
    patch(map_rows, 1, tiles - 2)
    lax.fori_loop(0, map_rows + 1, rim, 0)

    loads[0].wait()
    loads[1].wait()

    def far_first(step):
        return jnp.where(step < lats // 2, lats // 2 + step, lats - 1 - step)

    def partner(k):
        other = lat
        bit = 1
        while bit < lats:
            mine = lax.rem(lat // bit, 2)
            flip = lax.rem(k // bit, 2)
            other = other + bit * flip * (1 - 2 * mine)
            bit *= 2
        return other

    def sending_a(k):
        dest = partner(k)
        return pltpu.make_async_remote_copy(
            src_ref=out_a.at[dest],
            dst_ref=in_a.at[lat],
            send_sem=send_a.at[k],
            recv_sem=recv_a.at[k],
            device_id={"lat": dest, "lon": lon},
            device_id_type=MESH,
        )

    def stem(step, carry):
        k = far_first(step)
        dest = partner(k)
        first = pl.multiple_of(dest * width, width)
        here = xs[:, pl.ds(first, width + 8), :]
        x0 = here[:, :width, :].reshape((map_rows + 1) * width, depth).astype(jnp.bfloat16)
        x1 = here[:, 1 : width + 1, :].reshape((map_rows + 1) * width, depth).astype(jnp.bfloat16)
        count = map_rows * width
        total = jnp.dot(x0[:count], stem_w[0], preferred_element_type=jnp.float32)
        total += jnp.dot(x1[:count], stem_w[1], preferred_element_type=jnp.float32)
        total += jnp.dot(x0[width:], stem_w[2], preferred_element_type=jnp.float32)
        total += jnp.dot(x1[width:], stem_w[3], preferred_element_type=jnp.float32)
        found = jnp.maximum(total, 0.0).astype(jnp.bfloat16)
        feats[dest] = found
        middle = jnp.dot(found, down_w[...], preferred_element_type=jnp.float32)
        middle = jnp.maximum(middle, 0.0).astype(jnp.bfloat16)

        @pl.when(step < lats - 1)
        def _():
            out_a[dest] = middle
            sending_a(k).start()

        @pl.when(step == lats - 1)
        def _():
            in_a[lat] = middle

        return carry

    lax.fori_loop(0, lats, stem, 0)

    loads[2].wait()
    group = map_rows * width

    def project(k, carry):
        @pl.when(k > 0)
        def _():
            sending_a(k).wait()

        source = partner(k)
        found = jnp.dot(in_a[source], height_w[...], preferred_element_type=jnp.float32)
        at = pl.multiple_of(source * group, group)
        for c in range(proj_h.shape[0]):
            proj_h[c, pl.ds(at, group), :] = found[:, 128 * c : 128 * c + 128]
        return carry

    lax.fori_loop(0, lats, project, 0)
    beside = BLOCK // full_height
    part_width = width // HALVES
    home = lat * lons + lon
    column = lon * lats + lat

    def sending_b(h, step):
        k = far_first(step // lons)
        turn = lax.rem(step, lons)
        to_lat, to_lon = partner(k), lax.rem(lon + turn, lons)
        return pltpu.make_async_remote_copy(
            src_ref=out_b.at[h, to_lat * lons + to_lon],
            dst_ref=in_b.at[h, column],
            send_sem=send_b.at[h, step],
            recv_sem=recv_b.at[h, step],
            device_id={"lat": to_lat, "lon": to_lon},
            device_id_type=MESH,
        )

    own_step = others - lons

    def columns(h, carry):
        for b in range(part_width // beside):
            parts = []
            for w in range(beside):
                at = h * part_width + b * beside + w
                parts.append(
                    jnp.concatenate(
                        [
                            proj_h[c, pl.ds(at, full_height, stride=width), :]
                            for c in range(proj_h.shape[0])
                        ],
                        axis=1,
                    )
                )
            mine = jnp.concatenate(parts, axis=0).astype(jnp.bfloat16)
            out = attention(mine[:, :QK], mine[:, QK : 2 * QK], mine[:, 2 * QK :], bias_h)
            for w in range(beside):
                for c in range(result.shape[0]):
                    result[c, pl.ds(b * beside + w, full_height, stride=part_width), :] = out[
                        w * full_height : (w + 1) * full_height, 128 * c : 128 * c + 128
                    ]
        for c in range(result.shape[0]):
            out_b[h, :, :, 128 * c : 128 * c + 128] = (
                result[c].astype(jnp.bfloat16).reshape(others, own_rows * part_width, 128)
            )

        def start(step, carry):
            sending_b(h, step).start()
            return carry

        lax.fori_loop(0, own_step, start, 0)
        lax.fori_loop(own_step + 1, others, start, 0)
        in_b[h, column] = out_b[h, home]
        return carry

    lax.fori_loop(0, HALVES, columns, 0)

    loads[3].wait()

    def rows_in(h, carry):
        def finish(step, carry):
            sending_b(h, step).wait()
            return carry

        lax.fori_loop(0, own_step, finish, 0)
        lax.fori_loop(own_step + 1, others, finish, 0)
        found = jnp.dot(
            in_b[h].reshape(others * own_rows * part_width, VD),
            width_w[...],
            preferred_element_type=jnp.float32,
        ).reshape(others, own_rows, part_width, 2 * QK + VD)
        for r in range(own_rows):
            proj_w[r, :, h] = found[:, r]
        return carry

    lax.fori_loop(0, HALVES, rows_in, 0)

    def sending_c(r, k):
        there = lax.rem(lon + k, lons)
        return pltpu.make_async_remote_copy(
            src_ref=out_c.at[r, there],
            dst_ref=in_c.at[lon, r],
            send_sem=send_c.at[r, k],
            recv_sem=recv_c.at[r, k],
            device_id={"lat": lat, "lon": there},
            device_id_type=MESH,
        )

    def row(r, carry):
        mine = proj_w[r].reshape(full_width, 2 * QK + VD).astype(jnp.bfloat16)
        out = attention(mine[:, :QK], mine[:, QK : 2 * QK], mine[:, 2 * QK :], bias_w)
        out_c[r] = jnp.maximum(out, 0.0).astype(jnp.bfloat16).reshape(lons, map_cols, VD)

        def start(k, carry):
            sending_c(r, k).start()
            return carry

        lax.fori_loop(1, lons, start, 0)
        in_c[lon, r] = out_c[r, lon]
        return carry

    lax.fori_loop(0, own_rows, row, 0)

    loads[4].wait()

    def widen(k, carry):
        source = lax.rem(lon + lons - k, lons)

        @pl.when(k > 0)
        def _():
            for r in range(own_rows):
                sending_c(r, k).wait()

        x = in_c[source].reshape(own_rows * map_cols, VD)
        branch = jnp.dot(x, up_w[...], preferred_element_type=jnp.float32)
        for r in range(own_rows):
            for g in range(lats):
                at = pl.multiple_of((source * own_rows + r) * width, width)
                start = r * map_cols + g * width
                total = feats[g, pl.ds(at, width), :].astype(jnp.float32)
                total = jnp.maximum(total + branch[start : start + width], 0.0)
                out_ref[source * own_rows + r, g * width : (g + 1) * width, :] = total.astype(
                    jnp.bfloat16
                )
        return carry

    lax.fori_loop(0, lons, widen, 0)


def with_kernel(
    imagery, stem_weight, down_weight, height_qkv, height_bias, width_qkv, width_bias, up_weight
):
    lats, lons = lax.axis_size("lat"), lax.axis_size("lon")
    bf16, f32 = jnp.bfloat16, jnp.float32
    _, rows, cols = imagery.shape
    map_rows, map_cols = rows // PATCH, cols // PATCH
    positions = map_rows * map_cols
    depth, channels = stem_weight.shape[1:]
    full_width = map_cols * lons
    part_width = map_cols // lats // HALVES
    own_rows = map_rows // lons
    others = lats * lons
    qkv = 2 * QK + VD
    dma = pltpu.SemaphoreType.DMA
    exchange_a = pltpu.VMEM((lats, positions // lats, VD), bf16)
    exchange_b = pltpu.VMEM((HALVES, others, own_rows * part_width, VD), bf16)
    return pl.pallas_call(
        functools.partial(block_kernel, lats, lons),
        name="block",
        out_shape=jax.ShapeDtypeStruct((map_rows, map_cols, channels), bf16),
        in_specs=[ANY] * 6 + [VMEM] * 2,
        out_specs=VMEM,
        scratch_shapes=[
            pltpu.VMEM((3, rows + 32, cols + 256), bf16),
            pltpu.VMEM(stem_weight.shape, bf16),
            pltpu.VMEM(down_weight.shape, bf16),
            pltpu.VMEM(height_qkv.shape, bf16),
            pltpu.VMEM(width_qkv.shape, bf16),
            pltpu.VMEM(up_weight.shape, bf16),
            pltpu.VMEM((map_rows + 1, map_cols + 8, depth), f32),
            pltpu.VMEM((lats, positions // lats, channels), bf16),
            pltpu.VMEM((HEADS, BLOCK), f32),
            pltpu.VMEM((HEADS, BLOCK, BLOCK), f32),
            pltpu.VMEM((HEADS, full_width, full_width), f32),
            pltpu.VMEM((qkv // 128, positions, 128), f32),
            pltpu.VMEM((VD // 128, positions // HALVES, 128), f32),
            pltpu.VMEM((own_rows, others, HALVES, part_width, qkv), f32),
            exchange_a,
            exchange_a,
            exchange_b,
            exchange_b,
            pltpu.VMEM((own_rows, lons, map_cols, VD), bf16),
            pltpu.VMEM((lons, own_rows, map_cols, VD), bf16),
            dma((6,)),
            dma((8,)),
            dma((8,)),
            dma((lats,)),
            dma((lats,)),
            dma((HALVES, others)),
            dma((HALVES, others)),
            dma((own_rows, lons)),
            dma((own_rows, lons)),
        ],
        compiler_params=pltpu.CompilerParams(
            collective_id=0, has_side_effects=True, vmem_limit_bytes=VMEM_BYTES
        ),
    )(
        imagery, stem_weight, down_weight, height_qkv, width_qkv, up_weight, height_bias, width_bias
    )


def either(*args):
    lats, lons = lax.axis_size("lat"), lax.axis_size("lon")
    _, rows, cols = args[0].shape
    map_rows, map_cols = rows // PATCH, cols // PATCH
    height, width = map_rows * lats, map_cols // lats
    whole_tiles = (
        lats & (lats - 1) == 0
        and map_cols % (16 * lats) == 0
        and map_rows % lons == 0
        and 2 * height - 1 <= BLOCK
        and BLOCK % height == 0
        and width % (8 * HALVES) == 0
        and (width // HALVES) % (BLOCK // height) == 0
        and (map_rows // lons) * (width // HALVES) % 16 == 0
        and cols % 128 == 0
        and map_rows % 8 == 0
    )
    return with_kernel(*args) if whole_tiles else on_device(*args)


def solution(mesh):
    placed = (P("batch", "lat", "lon"), P(), P(), P(), P(), P(), P(), P())
    return jax.shard_map(
        either,
        mesh=mesh,
        in_specs=placed,
        out_specs=P(("batch", "lat"), "lon", None),
        check_vma=False,
    )
```

```python
import functools

import jax
import jax.numpy as jnp
from jax import lax
from jax.experimental import pallas as pl
from jax.experimental.pallas import tpu as pltpu
from jax.sharding import PartitionSpec as P

QK = 256
VD = 512
HEADS = 8
PATCH = 16
DQ = 32
DV = 64


lowest_score = -1e30


def extended(cells, sides, width, closed):
    for axis, dim in sides:
        count = lax.axis_size(axis)
        ends = count if closed else count - 1
        head = lax.slice_in_dim(cells, 0, width, axis=dim)
        tail = lax.slice_in_dim(cells, cells.shape[dim] - width, cells.shape[dim], axis=dim)
        cells = jnp.concatenate(
            [
                lax.ppermute(tail, axis, [(i, (i + 1) % count) for i in range(ends)]),
                cells,
                lax.ppermute(head, axis, [((i + 1) % count, i) for i in range(ends)]),
            ],
            axis=dim,
        )
    return cells


def stem_features(padded, stem_weight, map_rows, map_cols):
    channels = padded.shape[0]
    blocks = padded.reshape(channels, map_rows + 1, PATCH, map_cols + 1, PATCH)
    blocks = blocks.transpose(1, 3, 0, 2, 4).reshape(
        map_rows + 1, map_cols + 1, channels * PATCH * PATCH
    )
    summed = jnp.zeros((map_rows * map_cols, stem_weight.shape[2]), jnp.float32)
    for row_shift in range(2):
        for col_shift in range(2):
            window = blocks[row_shift : row_shift + map_rows, col_shift : col_shift + map_cols]
            window = window.reshape(map_rows * map_cols, channels * PATCH * PATCH)
            summed = summed + jnp.dot(
                window, stem_weight[2 * row_shift + col_shift], preferred_element_type=jnp.float32
            )
    return jax.nn.relu(summed).astype(jnp.bfloat16)


def online_update(carried, scores, value_heads, form):
    running_max, denominator, weighted = carried
    new_peak = jnp.maximum(running_max, jnp.max(scores, axis=-1))
    weights = jnp.exp(scores - new_peak[..., None])
    denominator = jnp.sum(weights, axis=-1)
    weighted = jnp.einsum(
        form, weights.astype(jnp.bfloat16), value_heads, preferred_element_type=jnp.float32
    )
    return (new_peak, denominator, weighted)


def on_device(
    imagery, stem_weight, down_weight, height_qkv, height_bias, width_qkv, width_bias, up_weight
):
    rim_width = PATCH // 2
    widened = extended(imagery, (("lon", 2),), rim_width, True)
    padded = extended(widened, (("lat", 1),), rim_width, False)
    map_rows = imagery.shape[1] // PATCH
    map_cols = imagery.shape[2] // PATCH
    full_height = map_rows * lax.axis_size("lat")
    full_width = map_cols * lax.axis_size("lon")
    row_first = lax.axis_index("lat") * map_rows
    col_first = lax.axis_index("lon") * map_cols
    score_scale = DQ ** (-0.5)
    features = stem_features(padded, stem_weight, map_rows, map_cols)
    middle = jax.nn.relu(jnp.dot(features, down_weight, preferred_element_type=jnp.float32)).astype(
        jnp.bfloat16
    )
    height_proj = jnp.dot(middle, height_qkv, preferred_element_type=jnp.float32).astype(
        jnp.bfloat16
    )
    height_proj = height_proj.reshape(map_rows, map_cols, 2 * QK + VD)
    height_queries = height_proj[..., :QK].reshape(map_rows, map_cols, HEADS, DQ)
    initial = (
        jnp.full((HEADS, map_cols, map_rows), lowest_score, jnp.float32),
        jnp.zeros((HEADS, map_cols, map_rows), jnp.float32),
        jnp.zeros((HEADS, map_cols, map_rows, DV), jnp.float32),
    )
    key_rows = lax.all_gather(height_proj[..., QK : 2 * QK], "lat", axis=0, tiled=True)
    value_rows = lax.all_gather(height_proj[..., 2 * QK :], "lat", axis=0, tiled=True)
    key_count = key_rows.shape[0]
    scores = (
        jnp.einsum(
            "pwnd,ownd->nwpo",
            height_queries,
            key_rows.reshape(key_count, map_cols, HEADS, DQ),
            preferred_element_type=jnp.float32,
        )
        * score_scale
    )
    offsets = (
        jnp.arange(key_count, dtype=jnp.int32)[None, :]
        - (row_first + jnp.arange(map_rows, dtype=jnp.int32))[:, None]
        + full_height
        - 1
    )
    scores = scores + jnp.take(height_bias, offsets, axis=1)[:, None]
    running_max, denominator, weighted = online_update(
        initial, scores, value_rows.reshape(key_count, map_cols, HEADS, DV), "nwpo,ownd->nwpd"
    )
    height_out = (
        (weighted / denominator[..., None])
        .transpose(2, 1, 0, 3)
        .reshape(map_rows, map_cols, VD)
        .astype(jnp.bfloat16)
    )
    width_proj = jnp.dot(
        height_out.reshape(map_rows * map_cols, VD), width_qkv, preferred_element_type=jnp.float32
    ).astype(jnp.bfloat16)
    width_proj = width_proj.reshape(map_rows, map_cols, 2 * QK + VD)
    width_queries = width_proj[..., :QK].reshape(map_rows, map_cols, HEADS, DQ)
    width_initial = (
        jnp.full((HEADS, map_rows, map_cols), lowest_score, jnp.float32),
        jnp.zeros((HEADS, map_rows, map_cols), jnp.float32),
        jnp.zeros((HEADS, map_rows, map_cols, DV), jnp.float32),
    )
    key_cols = lax.all_gather(width_proj[..., QK : 2 * QK], "lon", axis=1, tiled=True)
    value_cols = lax.all_gather(width_proj[..., 2 * QK :], "lon", axis=1, tiled=True)
    key_count = key_cols.shape[1]
    scores = (
        jnp.einsum(
            "hwnd,hknd->nhwk",
            width_queries,
            key_cols.reshape(map_rows, key_count, HEADS, DQ),
            preferred_element_type=jnp.float32,
        )
        * score_scale
    )
    offsets = (
        jnp.arange(key_count, dtype=jnp.int32)[None, :]
        - (col_first + jnp.arange(map_cols, dtype=jnp.int32))[:, None]
    ) % full_width
    scores = scores + jnp.take(width_bias, offsets, axis=1)[:, None]
    width_max, width_denominator, width_weighted = online_update(
        width_initial, scores, value_cols.reshape(map_rows, key_count, HEADS, DV), "nhwk,hknd->nhwd"
    )
    width_out = (
        (width_weighted / width_denominator[..., None])
        .transpose(1, 2, 0, 3)
        .reshape(map_rows * map_cols, VD)
        .astype(jnp.bfloat16)
    )
    branch = jnp.dot(jax.nn.relu(width_out), up_weight, preferred_element_type=jnp.float32)
    result = jax.nn.relu(features.astype(jnp.float32) + branch).astype(jnp.bfloat16)
    return result.reshape(map_rows, map_cols, up_weight.shape[1])


MESH = pl.DeviceIdType.MESH
ANY = pl.BlockSpec(memory_space=pl.ANY)
VMEM = pl.BlockSpec(memory_space=pltpu.VMEM)
BLOCK = 128
HALVES = 2
VMEM_BYTES = 58 * 1024 * 1024
LOG2E = 1.4426950408889634


def chunks_turned(tile, to_bands, pick, to_rows):
    turned = jnp.take_along_axis(tile, to_bands, axis=1, mode="promise_in_bounds")
    turned = jnp.take_along_axis(turned, pick, axis=0, mode="promise_in_bounds")
    return jnp.take_along_axis(turned, to_rows, axis=1, mode="promise_in_bounds")


def attention(q, k, v, bias):
    count = q.shape[0]
    lane = lax.broadcasted_iota(jnp.int32, (count, QK), 1) // DQ
    first = lax.broadcasted_iota(jnp.int32, (count, 2 * DV), 1) < DV
    outs = []
    for pair in range(HEADS // 2):
        values = v[:, 2 * DV * pair : 2 * DV * (pair + 1)]
        ones = jnp.ones_like(values)
        both = []
        for n in (2 * pair, 2 * pair + 1):
            q_head = jnp.where(lane == n, q, jnp.zeros_like(q))
            scores = lax.dot_general(
                q_head, k, (((1,), (1,)), ((), ())), preferred_element_type=jnp.float32
            )
            scores = scores * (DQ ** (-0.5) * LOG2E) + bias[n]
            weights = jnp.exp2(scores - jnp.max(scores, axis=-1, keepdims=True))
            held = jnp.where(first, values, ones) if n % 2 == 0 else jnp.where(first, ones, values)
            both.append(
                jnp.dot(weights.astype(jnp.bfloat16), held, preferred_element_type=jnp.float32)
            )
        totals = pltpu.roll(jnp.where(first, both[1], both[0]), DV, 1)
        outs.append(jnp.where(first, both[0], both[1]) / totals)
    return jnp.concatenate(outs, axis=1)


def block_kernel(
    lats, lons, img, stem_hbm, down_hbm, height_hbm, width_hbm, up_hbm, height_bias, width_bias,
    out_ref,
    ext, edge_out, edge_in, rim_out, rim_in, stem_w, down_w, height_w, width_w, up_w, xs, feats, padded_bias, bias_h, bias_w,
    proj_h, result, proj_w, out_a, in_a, out_b, in_b, out_c, in_c,
    load_sems, halo_send, halo_recv, send_a, recv_a, send_b, recv_b, send_c, recv_c,
):
    lat, lon = lax.axis_index("lat"), lax.axis_index("lon")
    rows, cols = img.shape[1], img.shape[2]
    map_rows, map_cols = rows // PATCH, cols // PATCH
    full_height, full_width = map_rows * lats, map_cols * lons
    width = map_cols // lats
    own_rows = map_rows // lons
    depth = 3 * PATCH * PATCH
    others = lats * lons

    barrier = pltpu.get_barrier_semaphore()

    def greet(step, carry):
        there = lax.rem(lon * lats + lat + step, others)
        pl.semaphore_signal(
            barrier,
            inc=1,
            device_id={"lat": lax.rem(there, lats), "lon": there // lats},
            device_id_type=MESH,
        )
        return carry

    lax.fori_loop(1, others, greet, 0)
    local = pltpu.make_async_copy(
        img, ext.at[:, pl.ds(16, rows), pl.ds(128, cols)], load_sems.at[0]
    )
    local.start()
    loads = []
    for number, (source, held) in enumerate(
        (
            (stem_hbm, stem_w),
            (down_hbm, down_w),
            (height_hbm, height_w),
            (width_hbm, width_w),
            (up_hbm, up_w),
        )
    ):
        loads.append(pltpu.make_async_copy(source, held, load_sems.at[number + 1]))
        loads[-1].start()
    west, east = lax.rem(lon + lons - 1, lons), lax.rem(lon + 1, lons)

    @pl.when(lat == 0)
    def _():
        rim_in[0] = jnp.zeros(rim_in.shape[1:], rim_in.dtype)
        edge_in[:, 0:16, :] = jnp.zeros((2, 16, 128), edge_in.dtype)

    @pl.when(lat == lats - 1)
    def _():
        rim_in[1] = jnp.zeros(rim_in.shape[1:], rim_in.dtype)
        edge_in[:, rows + 16 : rows + 32, :] = jnp.zeros((2, 16, 128), edge_in.dtype)

    local.wait()
    edge_lane = lax.broadcasted_iota(jnp.int32, (rows, 128), 1) // 8
    for side, at in ((0, 128), (1, cols)):
        packed = jnp.zeros((rows, 128), jnp.float32)
        for c in range(3):
            tile = ext[c, 16 : 16 + rows, at : at + 128].astype(jnp.float32)
            shift = 8 * c + 8 * side
            tile = pltpu.roll(tile, shift, 1) if shift else tile
            packed = jnp.where(edge_lane == c, tile, packed)
        edge_out[side] = packed.astype(jnp.bfloat16)
    half_row = cols // 2
    for side, at in ((0, 16), (1, rows)):
        for c in range(3):
            slab = ext[c, at : at + 16, 128 : 128 + cols].astype(jnp.float32)
            slab = slab[8 * side : 8 * side + 8]
            slab = jnp.concatenate([slab[:, :half_row], slab[:, half_row:]], axis=0)
            rim_out[side, c] = slab.astype(jnp.bfloat16)

    copies = []
    for down, right in ((0, -1), (0, 1), (-1, 0), (1, 0), (-1, -1), (-1, 1), (1, -1), (1, 1)):
        slot = len(copies)
        if right == 0:
            source = rim_out.at[(1 + down) // 2]
            target = rim_in.at[(1 - down) // 2]
        else:
            y_from, y_to, y_size = {
                -1: (0, rows + 16, 16), 0: (0, 16, rows), 1: (rows - 16, 0, 16)
            }[down]
            source = edge_out.at[(1 + right) // 2, pl.ds(y_from, y_size), :]
            target = edge_in.at[(1 - right) // 2, pl.ds(y_to, y_size), :]
        copy = pltpu.make_async_remote_copy(
            src_ref=source,
            dst_ref=target,
            send_sem=halo_send.at[slot],
            recv_sem=halo_recv.at[slot],
            device_id={
                "lat": lax.rem(lat + down + lats, lats),
                "lon": {-1: west, 0: lon, 1: east}[right],
            },
            device_id_type=MESH,
        )
        copies.append((down, copy))

    lane = lax.broadcasted_iota(jnp.int32, (8, 128), 1)
    sub = lax.broadcasted_iota(jnp.int32, (8, 128), 0)
    to_bands = lax.rem(lane - 16 * sub + 128, 128)
    pick = lax.rem(lane // 16 - sub + 8, 8)
    to_rows = lax.rem(lane + 16 * sub, 128)
    tiles = cols // 128 + 1

    def patch(i, first, count):
        for c in range(3):
            slab = ext[
                c,
                pl.ds(pl.multiple_of(16 * i, 16), 32),
                128 * first : 128 * (first + count + 1),
            ].astype(jnp.float32)
            for half in range(2):
                part = slab[8 + 8 * half : 16 + 8 * half, 120 : 120 + 128 * count]
                for t in range(count):
                    at = 8 * (first + t)
                    xs[i, at : at + 8, (2 * c + half) * 128 : (2 * c + half + 1) * 128] = (
                        chunks_turned(part[:, 128 * t : 128 * t + 128], to_bands, pick, to_rows)
                    )

    def inner(i, carry):
        patch(i, 1, tiles - 2)
        return carry

    def rim(i, carry):
        patch(i, 0, 1)
        patch(i, tiles - 1, 1)
        return carry

    lax.fori_loop(1, map_rows, inner, 0)
    pl.semaphore_wait(barrier, others - 1)
    for down, copy in copies:
        if down == 0:
            copy.start()
        elif down == -1:
            pl.when(lat > 0)(copy.start)
        else:
            pl.when(lat < lats - 1)(copy.start)

    padded_bias[...] = jnp.zeros(padded_bias.shape, jnp.float32)
    padded_bias[:, 0 : height_bias.shape[1]] = height_bias[...]
    down_row = lax.broadcasted_iota(jnp.int32, (BLOCK, BLOCK), 0) // full_height
    key_row = lax.broadcasted_iota(jnp.int32, (BLOCK, BLOCK), 1) // full_height
    for n in range(HEADS):
        spread = jnp.broadcast_to(padded_bias[n : n + 1, :] * LOG2E, (BLOCK, BLOCK))
        turned = pltpu.roll(spread, BLOCK - (full_height - 1), 1, stride=1, stride_axis=0)
        bias_h[n] = jnp.where(down_row == key_row, turned, lowest_score)
        spread = jnp.broadcast_to(width_bias[n : n + 1, :] * LOG2E, (full_width, full_width))
        bias_w[n] = pltpu.roll(spread, 0, 1, stride=1, stride_axis=0)

    for down, copy in copies:
        if down == 0:
            copy.wait_send()
            copy.wait_recv()
        elif down == -1:
            pl.when(lat > 0)(copy.wait_send)
            pl.when(lat < lats - 1)(copy.wait_recv)
        else:
            pl.when(lat < lats - 1)(copy.wait_send)
            pl.when(lat > 0)(copy.wait_recv)
    for c in range(3):
        for side, at in ((0, 0), (1, cols + 128)):
            tile = edge_in[side].astype(jnp.float32)
            shift = (128 - 8 * c - 8 * (1 - side)) % 128
            tile = pltpu.roll(tile, shift, 1) if shift else tile
            ext[c, :, at : at + 128] = tile.astype(jnp.bfloat16)
        for side, at in ((0, 0), (1, rows + 16)):
            slab = rim_in[side, c].astype(jnp.float32)
            slab = jnp.concatenate([slab[:8], slab[8:]], axis=1)
            blank = jnp.zeros_like(slab)
            slab = [blank, slab] if side == 0 else [slab, blank]
            ext[c, at : at + 16, 128 : 128 + cols] = jnp.concatenate(slab, axis=0).astype(
                jnp.bfloat16
            )
    patch(0, 1, tiles - 2)
    patch(map_rows, 1, tiles - 2)
    lax.fori_loop(0, map_rows + 1, rim, 0)

    loads[0].wait()
    loads[1].wait()

    def far_first(step):
        return jnp.where(step < lats // 2, lats // 2 + step, lats - 1 - step)

    def partner(k):
        other = lat
        bit = 1
        while bit < lats:
            mine = lax.rem(lat // bit, 2)
            flip = lax.rem(k // bit, 2)
            other = other + bit * flip * (1 - 2 * mine)
            bit *= 2
        return other

    part_width = width // HALVES
    count = map_rows * part_width

    def sending_a(h, k):
        dest = partner(k)
        return pltpu.make_async_remote_copy(
            src_ref=out_a.at[h, dest],
            dst_ref=in_a.at[h, lat],
            send_sem=send_a.at[h, k],
            recv_sem=recv_a.at[h, k],
            device_id={"lat": dest, "lon": lon},
            device_id_type=MESH,
        )

    def stem(step, carry):
        h = step // (lats // 2)
        ks = [far_first(2 * lax.rem(step, lats // 2) + n) for n in range(2)]
        dests = [partner(k) for k in ks]
        blocks = [[], [], [], []]
        for dest in dests:
            first = pl.multiple_of(dest * width + h * part_width, part_width)
            here = xs[:, pl.ds(first, part_width + 8), :]
            for shift in range(2):
                x = here[:, shift : shift + part_width, :]
                x = x.reshape((map_rows + 1) * part_width, depth)
                blocks[shift].append(x[:count].astype(jnp.bfloat16))
                blocks[2 + shift].append(x[part_width:].astype(jnp.bfloat16))
        total = jnp.zeros((2 * count, stem_w.shape[2]), jnp.float32)
        for quadrant in range(4):
            total += jnp.dot(
                jnp.concatenate(blocks[quadrant], axis=0),
                stem_w[quadrant],
                preferred_element_type=jnp.float32,
            )
        found = jnp.maximum(total, 0.0).astype(jnp.bfloat16)
        middle = jnp.dot(found, down_w[...], preferred_element_type=jnp.float32)
        middle = jnp.maximum(middle, 0.0).astype(jnp.bfloat16)
        for n in range(2):
            k, dest = ks[n], dests[n]
            mine = middle[n * count : (n + 1) * count]

            @pl.when(k > 0)
            def _():
                out_a[h, dest] = mine
                sending_a(h, k).start()

            @pl.when(k == 0)
            def _():
                in_a[h, lat] = mine

        for n in range(2):
            feats[dests[n], h] = found[n * count : (n + 1) * count].astype(jnp.float32)
        return carry

    lax.fori_loop(0, HALVES * lats // 2, stem, 0)

    loads[2].wait()
    beside = BLOCK // full_height
    home = lat * lons + lon
    column = lon * lats + lat

    def sending_b(h, step):
        k = far_first(step // lons)
        turn = lax.rem(step, lons)
        to_lat, to_lon = partner(k), lax.rem(lon + turn, lons)
        return pltpu.make_async_remote_copy(
            src_ref=out_b.at[h, to_lat * lons + to_lon],
            dst_ref=in_b.at[h, column],
            send_sem=send_b.at[h, step],
            recv_sem=recv_b.at[h, step],
            device_id={"lat": to_lat, "lon": to_lon},
            device_id_type=MESH,
        )

    own_step = others - lons

    def columns(h, carry):
        def arrived(k, carry):
            sending_a(h, k).wait()
            return carry

        lax.fori_loop(1, lats, arrived, 0)
        found = jnp.dot(
            in_a[h].reshape(lats * count, VD), height_w[...], preferred_element_type=jnp.float32
        )
        for c in range(proj_h.shape[0]):
            proj_h[c] = found[:, 128 * c : 128 * c + 128]
        for b in range(part_width // beside):
            parts = []
            for w in range(beside):
                at = b * beside + w
                parts.append(
                    jnp.concatenate(
                        [
                            proj_h[c, pl.ds(at, full_height, stride=part_width), :]
                            for c in range(proj_h.shape[0])
                        ],
                        axis=1,
                    )
                )
            mine = jnp.concatenate(parts, axis=0).astype(jnp.bfloat16)
            out = attention(mine[:, :QK], mine[:, QK : 2 * QK], mine[:, 2 * QK :], bias_h)
            for w in range(beside):
                for c in range(result.shape[0]):
                    result[c, pl.ds(b * beside + w, full_height, stride=part_width), :] = out[
                        w * full_height : (w + 1) * full_height, 128 * c : 128 * c + 128
                    ]
        for c in range(result.shape[0]):
            out_b[h, :, :, 128 * c : 128 * c + 128] = (
                result[c].astype(jnp.bfloat16).reshape(others, own_rows * part_width, 128)
            )

        def start(step, carry):
            sending_b(h, step).start()
            return carry

        lax.fori_loop(0, own_step, start, 0)
        lax.fori_loop(own_step + 1, others, start, 0)
        in_b[h, column] = out_b[h, home]
        return carry

    lax.fori_loop(0, HALVES, columns, 0)

    loads[3].wait()

    def rows_in(h, carry):
        def finish(step, carry):
            sending_b(h, step).wait()
            return carry

        lax.fori_loop(0, own_step, finish, 0)
        lax.fori_loop(own_step + 1, others, finish, 0)
        found = jnp.dot(
            in_b[h].reshape(others * own_rows * part_width, VD),
            width_w[...],
            preferred_element_type=jnp.float32,
        ).reshape(others, own_rows, part_width, 2 * QK + VD)
        for r in range(own_rows):
            proj_w[r, :, h] = found[:, r]
        return carry

    lax.fori_loop(0, HALVES, rows_in, 0)

    def sending_c(r, k):
        there = lax.rem(lon + k, lons)
        return pltpu.make_async_remote_copy(
            src_ref=out_c.at[r, there],
            dst_ref=in_c.at[lon, r],
            send_sem=send_c.at[r, k],
            recv_sem=recv_c.at[r, k],
            device_id={"lat": lat, "lon": there},
            device_id_type=MESH,
        )

    def row(r, carry):
        mine = proj_w[r].reshape(full_width, 2 * QK + VD).astype(jnp.bfloat16)
        out = attention(mine[:, :QK], mine[:, QK : 2 * QK], mine[:, 2 * QK :], bias_w)
        out_c[r] = jnp.maximum(out, 0.0).astype(jnp.bfloat16).reshape(lons, map_cols, VD)

        def start(k, carry):
            sending_c(r, k).start()
            return carry

        lax.fori_loop(1, lons, start, 0)
        in_c[lon, r] = out_c[r, lon]
        return carry

    lax.fori_loop(0, own_rows, row, 0)

    loads[4].wait()

    def widen(k, carry):
        source = lax.rem(lon + lons - k, lons)

        @pl.when(k > 0)
        def _():
            for r in range(own_rows):
                sending_c(r, k).wait()

        x = in_c[source].reshape(own_rows * map_cols, VD)
        branch = jnp.dot(x, up_w[...], preferred_element_type=jnp.float32)
        for r in range(own_rows):
            i = source * own_rows + r
            at = pl.multiple_of(i * part_width, part_width)
            kept = [
                feats[g, h, pl.ds(at, part_width), :] for g in range(lats) for h in range(HALVES)
            ]
            total = jnp.concatenate(kept, axis=0) + branch[r * map_cols : (r + 1) * map_cols]
            out_ref[i] = jnp.maximum(total, 0.0).astype(jnp.bfloat16)
        return carry

    lax.fori_loop(0, lons, widen, 0)


def with_kernel(
    imagery, stem_weight, down_weight, height_qkv, height_bias, width_qkv, width_bias, up_weight
):
    lats, lons = lax.axis_size("lat"), lax.axis_size("lon")
    bf16, f32 = jnp.bfloat16, jnp.float32
    _, rows, cols = imagery.shape
    map_rows, map_cols = rows // PATCH, cols // PATCH
    positions = map_rows * map_cols
    depth, channels = stem_weight.shape[1:]
    full_width = map_cols * lons
    part_width = map_cols // lats // HALVES
    own_rows = map_rows // lons
    others = lats * lons
    qkv = 2 * QK + VD
    dma = pltpu.SemaphoreType.DMA
    exchange_a = pltpu.VMEM((HALVES, lats, map_rows * part_width, VD), bf16)
    exchange_b = pltpu.VMEM((HALVES, others, own_rows * part_width, VD), bf16)
    return pl.pallas_call(
        functools.partial(block_kernel, lats, lons),
        name="block",
        out_shape=jax.ShapeDtypeStruct((map_rows, map_cols, channels), bf16),
        in_specs=[ANY] * 6 + [VMEM] * 2,
        out_specs=VMEM,
        scratch_shapes=[
            pltpu.VMEM((3, rows + 32, cols + 256), bf16),
            pltpu.VMEM((2, rows, 128), bf16),
            pltpu.VMEM((2, rows + 32, 128), bf16),
            pltpu.VMEM((2, 3, 16, cols // 2), bf16),
            pltpu.VMEM((2, 3, 16, cols // 2), bf16),
            pltpu.VMEM(stem_weight.shape, bf16),
            pltpu.VMEM(down_weight.shape, bf16),
            pltpu.VMEM(height_qkv.shape, bf16),
            pltpu.VMEM(width_qkv.shape, bf16),
            pltpu.VMEM(up_weight.shape, bf16),
            pltpu.VMEM((map_rows + 1, map_cols + 8, depth), f32),
            pltpu.VMEM((lats, HALVES, map_rows * part_width, channels), f32),
            pltpu.VMEM((HEADS, BLOCK), f32),
            pltpu.VMEM((HEADS, BLOCK, BLOCK), f32),
            pltpu.VMEM((HEADS, full_width, full_width), f32),
            pltpu.VMEM((qkv // 128, positions // HALVES, 128), f32),
            pltpu.VMEM((VD // 128, positions // HALVES, 128), f32),
            pltpu.VMEM((own_rows, others, HALVES, part_width, qkv), f32),
            exchange_a,
            exchange_a,
            exchange_b,
            exchange_b,
            pltpu.VMEM((own_rows, lons, map_cols, VD), bf16),
            pltpu.VMEM((lons, own_rows, map_cols, VD), bf16),
            dma((6,)),
            dma((8,)),
            dma((8,)),
            dma((HALVES, lats)),
            dma((HALVES, lats)),
            dma((HALVES, others)),
            dma((HALVES, others)),
            dma((own_rows, lons)),
            dma((own_rows, lons)),
        ],
        compiler_params=pltpu.CompilerParams(
            collective_id=0, has_side_effects=True, vmem_limit_bytes=VMEM_BYTES
        ),
    )(
        imagery, stem_weight, down_weight, height_qkv, width_qkv, up_weight, height_bias, width_bias
    )


def either(*args):
    lats, lons = lax.axis_size("lat"), lax.axis_size("lon")
    _, rows, cols = args[0].shape
    map_rows, map_cols = rows // PATCH, cols // PATCH
    height, width = map_rows * lats, map_cols // lats
    whole_tiles = (
        lats & (lats - 1) == 0
        and lats > 1
        and rows % 16 == 0
        and cols % 256 == 0
        and map_rows * (width // HALVES) % 16 == 0
        and map_cols % (16 * lats) == 0
        and map_rows % lons == 0
        and 2 * height - 1 <= BLOCK
        and BLOCK % height == 0
        and width % (8 * HALVES) == 0
        and (width // HALVES) % (BLOCK // height) == 0
        and (map_rows // lons) * (width // HALVES) % 16 == 0
        and cols % 128 == 0
        and map_rows % 8 == 0
    )
    return with_kernel(*args) if whole_tiles else on_device(*args)


def solution(mesh):
    placed = (P("batch", "lat", "lon"), P(), P(), P(), P(), P(), P(), P())
    return jax.shard_map(
        either,
        mesh=mesh,
        in_specs=placed,
        out_specs=P(("batch", "lat"), "lon", None),
        check_vma=False,
    )
```

```python
import functools

import jax
import jax.numpy as jnp
from jax import lax
from jax.experimental import pallas as pl
from jax.experimental.pallas import tpu as pltpu
from jax.sharding import PartitionSpec as P

QK = 256
VD = 512
HEADS = 8
PATCH = 16
DQ = 32
DV = 64


lowest_score = -1e30


def extended(cells, sides, width, closed):
    for axis, dim in sides:
        count = lax.axis_size(axis)
        ends = count if closed else count - 1
        head = lax.slice_in_dim(cells, 0, width, axis=dim)
        tail = lax.slice_in_dim(cells, cells.shape[dim] - width, cells.shape[dim], axis=dim)
        cells = jnp.concatenate(
            [
                lax.ppermute(tail, axis, [(i, (i + 1) % count) for i in range(ends)]),
                cells,
                lax.ppermute(head, axis, [((i + 1) % count, i) for i in range(ends)]),
            ],
            axis=dim,
        )
    return cells


def stem_features(padded, stem_weight, map_rows, map_cols):
    channels = padded.shape[0]
    blocks = padded.reshape(channels, map_rows + 1, PATCH, map_cols + 1, PATCH)
    blocks = blocks.transpose(1, 3, 0, 2, 4).reshape(
        map_rows + 1, map_cols + 1, channels * PATCH * PATCH
    )
    summed = jnp.zeros((map_rows * map_cols, stem_weight.shape[2]), jnp.float32)
    for row_shift in range(2):
        for col_shift in range(2):
            window = blocks[row_shift : row_shift + map_rows, col_shift : col_shift + map_cols]
            window = window.reshape(map_rows * map_cols, channels * PATCH * PATCH)
            summed = summed + jnp.dot(
                window, stem_weight[2 * row_shift + col_shift], preferred_element_type=jnp.float32
            )
    return jax.nn.relu(summed).astype(jnp.bfloat16)


def online_update(carried, scores, value_heads, form):
    running_max, denominator, weighted = carried
    new_peak = jnp.maximum(running_max, jnp.max(scores, axis=-1))
    weights = jnp.exp(scores - new_peak[..., None])
    denominator = jnp.sum(weights, axis=-1)
    weighted = jnp.einsum(
        form, weights.astype(jnp.bfloat16), value_heads, preferred_element_type=jnp.float32
    )
    return (new_peak, denominator, weighted)


def on_device(
    imagery, stem_weight, down_weight, height_qkv, height_bias, width_qkv, width_bias, up_weight
):
    rim_width = PATCH // 2
    widened = extended(imagery, (("lon", 2),), rim_width, True)
    padded = extended(widened, (("lat", 1),), rim_width, False)
    map_rows = imagery.shape[1] // PATCH
    map_cols = imagery.shape[2] // PATCH
    full_height = map_rows * lax.axis_size("lat")
    full_width = map_cols * lax.axis_size("lon")
    row_first = lax.axis_index("lat") * map_rows
    col_first = lax.axis_index("lon") * map_cols
    score_scale = DQ ** (-0.5)
    features = stem_features(padded, stem_weight, map_rows, map_cols)
    middle = jax.nn.relu(jnp.dot(features, down_weight, preferred_element_type=jnp.float32)).astype(
        jnp.bfloat16
    )
    height_proj = jnp.dot(middle, height_qkv, preferred_element_type=jnp.float32).astype(
        jnp.bfloat16
    )
    height_proj = height_proj.reshape(map_rows, map_cols, 2 * QK + VD)
    height_queries = height_proj[..., :QK].reshape(map_rows, map_cols, HEADS, DQ)
    initial = (
        jnp.full((HEADS, map_cols, map_rows), lowest_score, jnp.float32),
        jnp.zeros((HEADS, map_cols, map_rows), jnp.float32),
        jnp.zeros((HEADS, map_cols, map_rows, DV), jnp.float32),
    )
    key_rows = lax.all_gather(height_proj[..., QK : 2 * QK], "lat", axis=0, tiled=True)
    value_rows = lax.all_gather(height_proj[..., 2 * QK :], "lat", axis=0, tiled=True)
    key_count = key_rows.shape[0]
    scores = (
        jnp.einsum(
            "pwnd,ownd->nwpo",
            height_queries,
            key_rows.reshape(key_count, map_cols, HEADS, DQ),
            preferred_element_type=jnp.float32,
        )
        * score_scale
    )
    offsets = (
        jnp.arange(key_count, dtype=jnp.int32)[None, :]
        - (row_first + jnp.arange(map_rows, dtype=jnp.int32))[:, None]
        + full_height
        - 1
    )
    scores = scores + jnp.take(height_bias, offsets, axis=1)[:, None]
    running_max, denominator, weighted = online_update(
        initial, scores, value_rows.reshape(key_count, map_cols, HEADS, DV), "nwpo,ownd->nwpd"
    )
    height_out = (
        (weighted / denominator[..., None])
        .transpose(2, 1, 0, 3)
        .reshape(map_rows, map_cols, VD)
        .astype(jnp.bfloat16)
    )
    width_proj = jnp.dot(
        height_out.reshape(map_rows * map_cols, VD), width_qkv, preferred_element_type=jnp.float32
    ).astype(jnp.bfloat16)
    width_proj = width_proj.reshape(map_rows, map_cols, 2 * QK + VD)
    width_queries = width_proj[..., :QK].reshape(map_rows, map_cols, HEADS, DQ)
    width_initial = (
        jnp.full((HEADS, map_rows, map_cols), lowest_score, jnp.float32),
        jnp.zeros((HEADS, map_rows, map_cols), jnp.float32),
        jnp.zeros((HEADS, map_rows, map_cols, DV), jnp.float32),
    )
    key_cols = lax.all_gather(width_proj[..., QK : 2 * QK], "lon", axis=1, tiled=True)
    value_cols = lax.all_gather(width_proj[..., 2 * QK :], "lon", axis=1, tiled=True)
    key_count = key_cols.shape[1]
    scores = (
        jnp.einsum(
            "hwnd,hknd->nhwk",
            width_queries,
            key_cols.reshape(map_rows, key_count, HEADS, DQ),
            preferred_element_type=jnp.float32,
        )
        * score_scale
    )
    offsets = (
        jnp.arange(key_count, dtype=jnp.int32)[None, :]
        - (col_first + jnp.arange(map_cols, dtype=jnp.int32))[:, None]
    ) % full_width
    scores = scores + jnp.take(width_bias, offsets, axis=1)[:, None]
    width_max, width_denominator, width_weighted = online_update(
        width_initial, scores, value_cols.reshape(map_rows, key_count, HEADS, DV), "nhwk,hknd->nhwd"
    )
    width_out = (
        (width_weighted / width_denominator[..., None])
        .transpose(1, 2, 0, 3)
        .reshape(map_rows * map_cols, VD)
        .astype(jnp.bfloat16)
    )
    branch = jnp.dot(jax.nn.relu(width_out), up_weight, preferred_element_type=jnp.float32)
    result = jax.nn.relu(features.astype(jnp.float32) + branch).astype(jnp.bfloat16)
    return result.reshape(map_rows, map_cols, up_weight.shape[1])


MESH = pl.DeviceIdType.MESH
ANY = pl.BlockSpec(memory_space=pl.ANY)
VMEM = pl.BlockSpec(memory_space=pltpu.VMEM)
BLOCK = 128
HALVES = 2
VMEM_BYTES = 58 * 1024 * 1024
LOG2E = 1.4426950408889634


def attention(q, k, v, bias):
    count = q.shape[0]
    lane = lax.broadcasted_iota(jnp.int32, (count, QK), 1) // DQ
    first = lax.broadcasted_iota(jnp.int32, (count, 2 * DV), 1) < DV
    outs = []
    for pair in range(HEADS // 2):
        values = v[:, 2 * DV * pair : 2 * DV * (pair + 1)]
        ones = jnp.ones_like(values)
        both = []
        for n in (2 * pair, 2 * pair + 1):
            q_head = jnp.where(lane == n, q, jnp.zeros_like(q))
            scores = lax.dot_general(
                q_head, k, (((1,), (1,)), ((), ())), preferred_element_type=jnp.float32
            )
            scores = scores * (DQ ** (-0.5) * LOG2E) + bias[n]
            weights = jnp.exp2(scores - jnp.max(scores, axis=-1, keepdims=True))
            held = jnp.where(first, values, ones) if n % 2 == 0 else jnp.where(first, ones, values)
            both.append(
                jnp.dot(weights.astype(jnp.bfloat16), held, preferred_element_type=jnp.float32)
            )
        totals = pltpu.roll(jnp.where(first, both[1], both[0]), DV, 1)
        outs.append(jnp.where(first, both[0], both[1]) / totals)
    return jnp.concatenate(outs, axis=1)


def block_kernel(
    lats, lons, img, stem_hbm, down_hbm, height_hbm, width_hbm, up_hbm, height_bias, width_bias,
    out_ref,
    ext, edge_out, edge_in, rim_out, rim_in, stem_w, down_w, height_w, width_w, up_w, xs, feats, padded_bias, bias_h, bias_w,
    proj_h, result, proj_w, out_a, in_a, out_b, in_b, out_c, in_c,
    load_sems, halo_send, halo_recv, send_a, recv_a, send_b, recv_b, send_c, recv_c,
):
    lat, lon = lax.axis_index("lat"), lax.axis_index("lon")
    rows, cols = img.shape[1], img.shape[2]
    map_rows, map_cols = rows // PATCH, cols // PATCH
    full_height, full_width = map_rows * lats, map_cols * lons
    width = map_cols // lats
    own_rows = map_rows // lons
    depth = 3 * PATCH * PATCH
    others = lats * lons

    barrier = pltpu.get_barrier_semaphore()

    def greet(step, carry):
        there = lax.rem(lon * lats + lat + step, others)
        pl.semaphore_signal(
            barrier,
            inc=1,
            device_id={"lat": lax.rem(there, lats), "lon": there // lats},
            device_id_type=MESH,
        )
        return carry

    lax.fori_loop(1, others, greet, 0)
    local = pltpu.make_async_copy(
        img, ext.at[:, pl.ds(16, rows), pl.ds(128, cols)], load_sems.at[0]
    )
    local.start()
    loads = []
    for number, (source, held) in enumerate(
        (
            (stem_hbm, stem_w),
            (down_hbm, down_w),
            (height_hbm, height_w),
            (width_hbm, width_w),
            (up_hbm, up_w),
        )
    ):
        loads.append(pltpu.make_async_copy(source, held, load_sems.at[number + 1]))
        loads[-1].start()
    west, east = lax.rem(lon + lons - 1, lons), lax.rem(lon + 1, lons)

    @pl.when(lat == 0)
    def _():
        rim_in[0] = jnp.zeros(rim_in.shape[1:], rim_in.dtype)
        edge_in[:, 0:16, :] = jnp.zeros((2, 16, 128), edge_in.dtype)

    @pl.when(lat == lats - 1)
    def _():
        rim_in[1] = jnp.zeros(rim_in.shape[1:], rim_in.dtype)
        edge_in[:, rows + 16 : rows + 32, :] = jnp.zeros((2, 16, 128), edge_in.dtype)

    local.wait()
    edge_lane = lax.broadcasted_iota(jnp.int32, (rows, 128), 1) // 8
    for side, at in ((0, 128), (1, cols)):
        packed = jnp.zeros((rows, 128), jnp.float32)
        for c in range(3):
            tile = ext[c, 16 : 16 + rows, at : at + 128].astype(jnp.float32)
            shift = 8 * c + 8 * side
            tile = pltpu.roll(tile, shift, 1) if shift else tile
            packed = jnp.where(edge_lane == c, tile, packed)
        edge_out[side] = packed.astype(jnp.bfloat16)
    half_row = cols // 2
    for side, at in ((0, 16), (1, rows)):
        for c in range(3):
            slab = ext[c, at : at + 16, 128 : 128 + cols].astype(jnp.float32)
            slab = slab[8 * side : 8 * side + 8]
            slab = jnp.concatenate([slab[:, :half_row], slab[:, half_row:]], axis=0)
            rim_out[side, c] = slab.astype(jnp.bfloat16)

    copies = []
    for down, right in ((0, -1), (0, 1), (-1, 0), (1, 0), (-1, -1), (-1, 1), (1, -1), (1, 1)):
        slot = len(copies)
        if right == 0:
            source = rim_out.at[(1 + down) // 2]
            target = rim_in.at[(1 - down) // 2]
        else:
            y_from, y_to, y_size = {
                -1: (0, rows + 16, 16), 0: (0, 16, rows), 1: (rows - 16, 0, 16)
            }[down]
            source = edge_out.at[(1 + right) // 2, pl.ds(y_from, y_size), :]
            target = edge_in.at[(1 - right) // 2, pl.ds(y_to, y_size), :]
        copy = pltpu.make_async_remote_copy(
            src_ref=source,
            dst_ref=target,
            send_sem=halo_send.at[slot],
            recv_sem=halo_recv.at[slot],
            device_id={
                "lat": lax.rem(lat + down + lats, lats),
                "lon": {-1: west, 0: lon, 1: east}[right],
            },
            device_id_type=MESH,
        )
        copies.append((down, copy))

    lane = lax.broadcasted_iota(jnp.int32, (8, 128), 1)
    sub = lax.broadcasted_iota(jnp.int32, (8, 128), 0)
    to_bands = lax.rem(lane - 16 * sub + 128, 128)
    pick = lax.rem(lane // 16 - sub + 8, 8)
    to_rows = lax.rem(lane + 16 * sub, 128)
    from_bands = lax.rem(to_bands + 120, 128)
    taken = functools.partial(jnp.take_along_axis, mode="promise_in_bounds")
    tiles = cols // 128 + 1

    def patch(i, first, count):
        for c in range(3):
            slab = ext[
                c,
                pl.ds(pl.multiple_of(16 * i, 16), 32),
                128 * first : 128 * (first + count + 1),
            ].astype(jnp.float32)
            for half in range(2):
                part = slab[8 + 8 * half : 16 + 8 * half]
                bands = [
                    taken(part[:, 128 * t : 128 * t + 128], from_bands, axis=1) for t in range(count + 1)
                ]
                for t in range(count):
                    at = 8 * (first + t)
                    tile = taken(jnp.where(to_bands < 8, bands[t], bands[t + 1]), pick, axis=0)
                    xs[i, at : at + 8, (2 * c + half) * 128 : (2 * c + half + 1) * 128] = taken(
                        tile, to_rows, axis=1
                    )

    def inner(i, carry):
        patch(i, 1, tiles - 2)
        return carry

    def rim(i, carry):
        patch(i, 0, 1)
        patch(i, tiles - 1, 1)
        return carry

    pl.semaphore_wait(barrier, others - 1)
    for down, copy in copies:
        if down == 0:
            copy.start()
        elif down == -1:
            pl.when(lat > 0)(copy.start)
        else:
            pl.when(lat < lats - 1)(copy.start)

    lax.fori_loop(1, map_rows, inner, 0)

    padded_bias[...] = jnp.zeros(padded_bias.shape, jnp.float32)
    padded_bias[:, 0 : height_bias.shape[1]] = height_bias[...]
    down_row = lax.broadcasted_iota(jnp.int32, (BLOCK, BLOCK), 0) // full_height
    key_row = lax.broadcasted_iota(jnp.int32, (BLOCK, BLOCK), 1) // full_height
    for n in range(HEADS):
        spread = jnp.broadcast_to(padded_bias[n : n + 1, :] * LOG2E, (BLOCK, BLOCK))
        turned = pltpu.roll(spread, BLOCK - (full_height - 1), 1, stride=1, stride_axis=0)
        bias_h[n] = jnp.where(down_row == key_row, turned, lowest_score)
        spread = jnp.broadcast_to(width_bias[n : n + 1, :] * LOG2E, (full_width, full_width))
        bias_w[n] = pltpu.roll(spread, 0, 1, stride=1, stride_axis=0)

    for down, copy in copies:
        if down == 0:
            copy.wait_send()
            copy.wait_recv()
        elif down == -1:
            pl.when(lat > 0)(copy.wait_send)
            pl.when(lat < lats - 1)(copy.wait_recv)
        else:
            pl.when(lat < lats - 1)(copy.wait_send)
            pl.when(lat > 0)(copy.wait_recv)
    for c in range(3):
        for side, at in ((0, 0), (1, cols + 128)):
            tile = edge_in[side].astype(jnp.float32)
            shift = (128 - 8 * c - 8 * (1 - side)) % 128
            tile = pltpu.roll(tile, shift, 1) if shift else tile
            ext[c, :, at : at + 128] = tile.astype(jnp.bfloat16)
        for side, at in ((0, 0), (1, rows + 16)):
            slab = rim_in[side, c].astype(jnp.float32)
            slab = jnp.concatenate([slab[:8], slab[8:]], axis=1)
            blank = jnp.zeros_like(slab)
            slab = [blank, slab] if side == 0 else [slab, blank]
            ext[c, at : at + 16, 128 : 128 + cols] = jnp.concatenate(slab, axis=0).astype(
                jnp.bfloat16
            )
    patch(0, 1, tiles - 2)
    patch(map_rows, 1, tiles - 2)
    lax.fori_loop(0, map_rows + 1, rim, 0)

    loads[0].wait()
    loads[1].wait()

    def far_first(step):
        return jnp.where(step < lats // 2, lats // 2 + step, lats - 1 - step)

    def partner(k):
        other = lat
        bit = 1
        while bit < lats:
            mine = lax.rem(lat // bit, 2)
            flip = lax.rem(k // bit, 2)
            other = other + bit * flip * (1 - 2 * mine)
            bit *= 2
        return other

    part_width = width // HALVES
    count = map_rows * part_width

    def sending_a(h, k):
        dest = partner(k)
        return pltpu.make_async_remote_copy(
            src_ref=out_a.at[h, dest],
            dst_ref=in_a.at[h, lat],
            send_sem=send_a.at[h, k],
            recv_sem=recv_a.at[h, k],
            device_id={"lat": dest, "lon": lon},
            device_id_type=MESH,
        )

    def stem(step, carry):
        h = step // (lats // 2)
        ks = [far_first(2 * lax.rem(step, lats // 2) + n) for n in range(2)]
        dests = [partner(k) for k in ks]
        blocks = [[], [], [], []]
        for dest in dests:
            first = pl.multiple_of(dest * width + h * part_width, part_width)
            here = xs[:, pl.ds(first, part_width + 8), :]
            for shift in range(2):
                x = here[:, shift : shift + part_width, :]
                x = x.reshape((map_rows + 1) * part_width, depth)
                blocks[shift].append(x[:count].astype(jnp.bfloat16))
                blocks[2 + shift].append(x[part_width:].astype(jnp.bfloat16))
        total = jnp.zeros((2 * count, stem_w.shape[2]), jnp.float32)
        for quadrant in range(4):
            total += jnp.dot(
                jnp.concatenate(blocks[quadrant], axis=0),
                stem_w[quadrant],
                preferred_element_type=jnp.float32,
            )
        found = jnp.maximum(total, 0.0).astype(jnp.bfloat16)
        middle = jnp.dot(found, down_w[...], preferred_element_type=jnp.float32)
        middle = jnp.maximum(middle, 0.0).astype(jnp.bfloat16)
        for n in range(2):
            k, dest = ks[n], dests[n]
            mine = middle[n * count : (n + 1) * count]

            @pl.when(k > 0)
            def _():
                out_a[h, dest] = mine
                sending_a(h, k).start()

            @pl.when(k == 0)
            def _():
                in_a[h, lat] = mine

        for n in range(2):
            feats[dests[n], h] = found[n * count : (n + 1) * count].astype(jnp.float32)
        return carry

    lax.fori_loop(0, HALVES * lats // 2, stem, 0)

    loads[2].wait()
    beside = BLOCK // full_height
    home = lat * lons + lon
    column = lon * lats + lat

    def sending_b(h, step):
        k = far_first(step // lons)
        turn = lax.rem(step, lons)
        to_lat, to_lon = partner(k), lax.rem(lon + turn, lons)
        return pltpu.make_async_remote_copy(
            src_ref=out_b.at[h, to_lat * lons + to_lon],
            dst_ref=in_b.at[h, column],
            send_sem=send_b.at[h, step],
            recv_sem=recv_b.at[h, step],
            device_id={"lat": to_lat, "lon": to_lon},
            device_id_type=MESH,
        )

    own_step = others - lons

    def columns(h, carry):
        def arrived(k, carry):
            sending_a(h, k).wait()
            return carry

        lax.fori_loop(1, lats, arrived, 0)
        found = jnp.dot(
            in_a[h].reshape(lats * count, VD), height_w[...], preferred_element_type=jnp.float32
        )
        for c in range(proj_h.shape[0]):
            proj_h[c] = found[:, 128 * c : 128 * c + 128]
        for b in range(part_width // beside):
            parts = []
            for w in range(beside):
                at = b * beside + w
                parts.append(
                    jnp.concatenate(
                        [
                            proj_h[c, pl.ds(at, full_height, stride=part_width), :]
                            for c in range(proj_h.shape[0])
                        ],
                        axis=1,
                    )
                )
            mine = jnp.concatenate(parts, axis=0).astype(jnp.bfloat16)
            out = attention(mine[:, :QK], mine[:, QK : 2 * QK], mine[:, 2 * QK :], bias_h)
            for w in range(beside):
                for c in range(result.shape[0]):
                    result[c, pl.ds(b * beside + w, full_height, stride=part_width), :] = out[
                        w * full_height : (w + 1) * full_height, 128 * c : 128 * c + 128
                    ]
        for c in range(result.shape[0]):
            out_b[h, :, :, 128 * c : 128 * c + 128] = (
                result[c].astype(jnp.bfloat16).reshape(others, own_rows * part_width, 128)
            )

        def start(step, carry):
            sending_b(h, step).start()
            return carry

        lax.fori_loop(0, own_step, start, 0)
        lax.fori_loop(own_step + 1, others, start, 0)
        in_b[h, column] = out_b[h, home]
        return carry

    lax.fori_loop(0, HALVES, columns, 0)

    loads[3].wait()

    def rows_in(h, carry):
        def finish(step, carry):
            sending_b(h, step).wait()
            return carry

        lax.fori_loop(0, own_step, finish, 0)
        lax.fori_loop(own_step + 1, others, finish, 0)
        found = jnp.dot(
            in_b[h].reshape(others * own_rows * part_width, VD),
            width_w[...],
            preferred_element_type=jnp.float32,
        ).reshape(others, own_rows, part_width, 2 * QK + VD)
        for r in range(own_rows):
            proj_w[r, :, h] = found[:, r]
        return carry

    lax.fori_loop(0, HALVES, rows_in, 0)

    def sending_c(r, k):
        there = lax.rem(lon + k, lons)
        return pltpu.make_async_remote_copy(
            src_ref=out_c.at[r, there],
            dst_ref=in_c.at[lon, r],
            send_sem=send_c.at[r, k],
            recv_sem=recv_c.at[r, k],
            device_id={"lat": lat, "lon": there},
            device_id_type=MESH,
        )

    def row(r, carry):
        mine = proj_w[r].reshape(full_width, 2 * QK + VD).astype(jnp.bfloat16)
        out = attention(mine[:, :QK], mine[:, QK : 2 * QK], mine[:, 2 * QK :], bias_w)
        out_c[r] = jnp.maximum(out, 0.0).astype(jnp.bfloat16).reshape(lons, map_cols, VD)

        def start(k, carry):
            sending_c(r, k).start()
            return carry

        lax.fori_loop(1, lons, start, 0)
        in_c[lon, r] = out_c[r, lon]
        return carry

    lax.fori_loop(0, own_rows, row, 0)

    loads[4].wait()

    def widen(k, carry):
        source = lax.rem(lon + lons - k, lons)

        @pl.when(k > 0)
        def _():
            for r in range(own_rows):
                sending_c(r, k).wait()

        x = in_c[source].reshape(own_rows * map_cols, VD)
        branch = jnp.dot(x, up_w[...], preferred_element_type=jnp.float32)
        for r in range(own_rows):
            i = source * own_rows + r
            at = pl.multiple_of(i * part_width, part_width)
            kept = [
                feats[g, h, pl.ds(at, part_width), :] for g in range(lats) for h in range(HALVES)
            ]
            total = jnp.concatenate(kept, axis=0) + branch[r * map_cols : (r + 1) * map_cols]
            out_ref[i] = jnp.maximum(total, 0.0).astype(jnp.bfloat16)
        return carry

    lax.fori_loop(0, lons, widen, 0)


def with_kernel(
    imagery, stem_weight, down_weight, height_qkv, height_bias, width_qkv, width_bias, up_weight
):
    lats, lons = lax.axis_size("lat"), lax.axis_size("lon")
    bf16, f32 = jnp.bfloat16, jnp.float32
    _, rows, cols = imagery.shape
    map_rows, map_cols = rows // PATCH, cols // PATCH
    positions = map_rows * map_cols
    depth, channels = stem_weight.shape[1:]
    full_width = map_cols * lons
    part_width = map_cols // lats // HALVES
    own_rows = map_rows // lons
    others = lats * lons
    qkv = 2 * QK + VD
    dma = pltpu.SemaphoreType.DMA
    exchange_a = pltpu.VMEM((HALVES, lats, map_rows * part_width, VD), bf16)
    exchange_b = pltpu.VMEM((HALVES, others, own_rows * part_width, VD), bf16)
    return pl.pallas_call(
        functools.partial(block_kernel, lats, lons),
        name="block",
        out_shape=jax.ShapeDtypeStruct((map_rows, map_cols, channels), bf16),
        in_specs=[ANY] * 6 + [VMEM] * 2,
        out_specs=VMEM,
        scratch_shapes=[
            pltpu.VMEM((3, rows + 32, cols + 256), bf16),
            pltpu.VMEM((2, rows, 128), bf16),
            pltpu.VMEM((2, rows + 32, 128), bf16),
            pltpu.VMEM((2, 3, 16, cols // 2), bf16),
            pltpu.VMEM((2, 3, 16, cols // 2), bf16),
            pltpu.VMEM(stem_weight.shape, bf16),
            pltpu.VMEM(down_weight.shape, bf16),
            pltpu.VMEM(height_qkv.shape, bf16),
            pltpu.VMEM(width_qkv.shape, bf16),
            pltpu.VMEM(up_weight.shape, bf16),
            pltpu.VMEM((map_rows + 1, map_cols + 8, depth), f32),
            pltpu.VMEM((lats, HALVES, map_rows * part_width, channels), f32),
            pltpu.VMEM((HEADS, BLOCK), f32),
            pltpu.VMEM((HEADS, BLOCK, BLOCK), f32),
            pltpu.VMEM((HEADS, full_width, full_width), f32),
            pltpu.VMEM((qkv // 128, positions // HALVES, 128), f32),
            pltpu.VMEM((VD // 128, positions // HALVES, 128), f32),
            pltpu.VMEM((own_rows, others, HALVES, part_width, qkv), f32),
            exchange_a,
            exchange_a,
            exchange_b,
            exchange_b,
            pltpu.VMEM((own_rows, lons, map_cols, VD), bf16),
            pltpu.VMEM((lons, own_rows, map_cols, VD), bf16),
            dma((6,)),
            dma((8,)),
            dma((8,)),
            dma((HALVES, lats)),
            dma((HALVES, lats)),
            dma((HALVES, others)),
            dma((HALVES, others)),
            dma((own_rows, lons)),
            dma((own_rows, lons)),
        ],
        compiler_params=pltpu.CompilerParams(
            collective_id=0, has_side_effects=True, vmem_limit_bytes=VMEM_BYTES
        ),
    )(
        imagery, stem_weight, down_weight, height_qkv, width_qkv, up_weight, height_bias, width_bias
    )


def either(*args):
    lats, lons = lax.axis_size("lat"), lax.axis_size("lon")
    _, rows, cols = args[0].shape
    map_rows, map_cols = rows // PATCH, cols // PATCH
    height, width = map_rows * lats, map_cols // lats
    whole_tiles = (
        lats & (lats - 1) == 0
        and lats > 1
        and rows % 16 == 0
        and cols % 256 == 0
        and map_rows * (width // HALVES) % 16 == 0
        and map_cols % (16 * lats) == 0
        and map_rows % lons == 0
        and 2 * height - 1 <= BLOCK
        and BLOCK % height == 0
        and width % (8 * HALVES) == 0
        and (width // HALVES) % (BLOCK // height) == 0
        and (map_rows // lons) * (width // HALVES) % 16 == 0
        and cols % 128 == 0
        and map_rows % 8 == 0
    )
    return with_kernel(*args) if whole_tiles else on_device(*args)


def solution(mesh):
    placed = (P("batch", "lat", "lon"), P(), P(), P(), P(), P(), P(), P())
    return jax.shard_map(
        either,
        mesh=mesh,
        in_specs=placed,
        out_specs=P(("batch", "lat"), "lon", None),
        check_vma=False,
    )
```
